128 devices in a mesh: loader: 8 (over z, core), bucket: 16 (over x, y).
Axes of the slice: x: 4, y: 4, z: 4, core: 2. Of those that a mesh axis runs over, the one named last changes fastest.
Arguments:
- latents: bfloat16 [1024, 512], P(('loader', 'bucket')), may hold values from -6 to 6
- cotangent: bfloat16 [1024, 12288], P(('loader', 'bucket')), may hold values from -6 to 6
- frames: int32 [1024], P(('loader', 'bucket')), may hold values from 1 to 2
- heights: int32 [1024], P(('loader', 'bucket')), may hold values from 1 to 4
- widths: int32 [1024], P(('loader', 'bucket')), may hold values from 1 to 4
- bucket_ids: int32 [1024], P(('loader', 'bucket')), may hold values from 0 to 15, as said below
- w_in: bfloat16 [432, 384], replicated, may hold values from -0.3125 to 0.3125
- w_mid: bfloat16 [10368, 384], replicated, may hold values from -0.0625 to 0.0625
Outputs:
- decoded: bfloat16 [4096, 12288], P(('loader', 'bucket'))
- grad_in: float32 [165888], P(('loader', 'bucket'))
- grad_mid: float32 [3981312], P(('loader', 'bucket'))
The draws below stay inside these ranges and needn't reach their ends.
Inputs may be any that keep to these rules, and one draw needn't show every extreme that they name: `bucket_ids`: among the tiles of one device at most 2 have one bucket id; in every group along the loader axis one bucket receives exactly 2 tiles from every device of the group.
All inputs are finite; a program needn't handle non-finite values.
Results may differ from the reference program's by a relative error of at most 0.0034.
Values may be sent and summed in bfloat16 or wider, within the bound.
A program may use at most 192 MiB of HBM per device.

```python
import jax
import jax.numpy as jnp
from jax import lax

Z = 16
C = 384
TAPS = 27
TF = 2
TH = 4
TW = 4
TILES_DEV = 8
CAP = 2
P_SIZE = 32
TILES = 1024
SLOTS = 4096
N_LOADER = 8
N_BUCKET = 16


def draw_bucket_ids(key, part):
    key = jax.random.fold_in(key, 7)
    hot_key, rest_key, order_key = jax.random.split(key, 3)
    devices = N_LOADER * N_BUCKET
    hot = jax.random.randint(hot_key, (N_LOADER,), 0, N_BUCKET)
    hot_dev = jnp.repeat(hot, N_BUCKET)
    perms = jax.vmap(lambda single: jax.random.permutation(single, N_BUCKET))(jax.random.split(rest_key, devices))
    is_hot = (perms == hot_dev[:, None]).astype(jnp.int32)
    order = jnp.argsort(is_hot, axis=1, stable=True)
    others = jnp.take_along_axis(perms, order, axis=1)[:, :TILES_DEV - CAP]
    chosen = jnp.concatenate([jnp.broadcast_to(hot_dev[:, None], (devices, CAP)), others], axis=1)
    shuffled = jax.vmap(lambda single, row: jax.random.permutation(single, row))(jax.random.split(order_key, devices), chosen)
    return shuffled.reshape(-1).astype(jnp.int32)


def place_ends(drawn, stream_key, smallest, largest):
    shape = drawn.shape
    place = [jax.random.randint(jax.random.fold_in(stream_key, axis), (), 0, shape[axis]) for axis in range(len(shape))]
    drawn = drawn.at[tuple(place)].set(smallest)
    longest = shape.index(max(shape))
    place[longest] = (place[longest] + 1) % shape[longest]
    return drawn.at[tuple(place)].set(largest)


def block_levels(own_key, dims, cuts, least, largest):
    def one(dim, blocks):
        steps = jax.random.uniform(jax.random.fold_in(jax.random.fold_in(own_key, 6), dim), (blocks,), jnp.float32, least / len(cuts), largest / len(cuts))
        return jnp.repeat(jnp.exp(steps), dims[dim] // blocks).reshape((-1,) + (1,) * (len(dims) - dim - 1))

    loudness = one(*cuts[0])
    for cut in cuts[1:]:
        loudness = loudness * one(*cut)
    return loudness


def scatter_about(rng, extent, width, reach, shards=(), kind=jnp.bfloat16):
    array = jax.random.normal(rng, extent, jnp.float32) * width
    if len(shards) > 0:
        array = block_levels(rng, extent, shards, -0.22, 0.18) * array
    return jnp.clip(array, min=-reach, max=reach).astype(kind)


def setup_inputs(seed: int = 0) -> dict:
    streams_of = jax.random.split(jax.random.key(seed), 9)
    latents = scatter_about(streams_of[0], (TILES, P_SIZE * Z), 1.0, 6.0, ((0, 128),))
    cotangent = scatter_about(streams_of[1], (TILES, P_SIZE * C), 1.0, 6.0, ((0, 128),))
    frames = place_ends(jax.random.randint(streams_of[2], (TILES,), 1, TF + 1), jax.random.fold_in(streams_of[2], 1), 1, TF).astype(jnp.int32)
    heights = place_ends(jax.random.randint(streams_of[3], (TILES,), 1, TH + 1), jax.random.fold_in(streams_of[3], 1), 1, TH).astype(jnp.int32)
    widths = place_ends(jax.random.randint(streams_of[4], (TILES,), 1, TW + 1), jax.random.fold_in(streams_of[4], 1), 1, TW).astype(jnp.int32)
    bucket_ids = draw_bucket_ids(jax.random.fold_in(streams_of[8], 71), 0)
    w_in = scatter_about(streams_of[6], (TAPS * Z, C), (TAPS * Z) ** -0.5, 0.3125)
    w_mid = scatter_about(streams_of[7], (TAPS * C, C), (TAPS * C) ** -0.5, 0.0625)
    return dict(latents=latents, cotangent=cotangent, frames=frames, heights=heights, widths=widths, bucket_ids=bucket_ids, w_in=w_in, w_mid=w_mid)


def tile_mask(frames, heights, widths):
    fpos = jnp.arange(TF)[None, :, None, None]
    rpos = jnp.arange(TH)[None, None, :, None]
    cpos = jnp.arange(TW)[None, None, None, :]
    inside = (fpos < frames[:, None, None, None]) & (rpos < heights[:, None, None, None]) & (cpos < widths[:, None, None, None])
    return inside.astype(jnp.float32)[..., None]

def patches(field, flipped):
    if flipped:
        padded = jnp.pad(field, ((0, 0), (0, 2), (1, 1), (1, 1), (0, 0)))
    else:
        padded = jnp.pad(field, ((0, 0), (2, 0), (1, 1), (1, 1), (0, 0)))
    pieces = []
    for first in range(3):
        for second in range(3):
            for third in range(3):
                if flipped:
                    fa, fb, fc = (2 - first, 2 - second, 2 - third)
                else:
                    fa, fb, fc = (first, second, third)
                pieces.append(padded[:, fa:fa + TF, fb:fb + TH, fc:fc + TW, :])
    stacked = jnp.concatenate(pieces, axis=-1)
    return stacked.reshape(-1, stacked.shape[-1])

def decode_tiles(latent_rows, cot_rows, frames, heights, widths, w_in, w_mid):
    count = latent_rows.shape[0]
    mask = tile_mask(frames, heights, widths)
    flat_mask = mask.reshape(-1, 1)
    inputs = (latent_rows.reshape(count, TF, TH, TW, Z).astype(jnp.float32) * mask).astype(jnp.bfloat16)
    in_patch = patches(inputs, False)
    hidden = jnp.dot(in_patch, w_in, preferred_element_type=jnp.float32)
    scale_rows = lax.rsqrt(lax.optimization_barrier(jnp.mean(hidden * hidden, axis=-1, keepdims=True)) + 1e-06)
    normed = hidden * scale_rows
    sig = jax.nn.sigmoid(normed)
    active = (normed * sig).astype(jnp.bfloat16)
    mid_patch = patches(active.reshape(count, TF, TH, TW, C), False)
    output = hidden + jnp.dot(mid_patch, w_mid, preferred_element_type=jnp.float32)
    decoded_rows = (output * flat_mask).astype(jnp.bfloat16).reshape(count, TF * TH * TW * C)
    grad_out = jnp.where(flat_mask > 0, cot_rows.reshape(-1, C), jnp.zeros((), jnp.bfloat16))
    grad_mid = lax.dot_general(mid_patch, grad_out, (((0,), (0,)), ((), ())), preferred_element_type=jnp.float32)
    w_flip = jnp.transpose(w_mid.reshape(TAPS, C, C), (0, 2, 1)).reshape(TAPS * C, C)
    back_patch = patches(grad_out.reshape(count, TF, TH, TW, C), True)
    grad_act = jnp.dot(back_patch, w_flip, preferred_element_type=jnp.float32)
    grad_norm = grad_act * sig * (1.0 + normed * (1.0 - sig))
    grad_hidden = grad_out.astype(jnp.float32) + scale_rows * (grad_norm - normed * lax.optimization_barrier(jnp.mean(grad_norm * normed, axis=-1, keepdims=True)))
    grad_in = lax.dot_general(in_patch, grad_hidden.astype(jnp.bfloat16), (((0,), (0,)), ((), ())), preferred_element_type=jnp.float32)
    return (decoded_rows, grad_in, grad_mid)

def reference(latents, cotangent, frames, heights, widths, bucket_ids, w_in, w_mid):
    devices = N_LOADER * N_BUCKET
    blocks = (latents.reshape(devices, TILES_DEV, -1), cotangent.reshape(devices, TILES_DEV, -1), frames.reshape(devices, TILES_DEV), heights.reshape(devices, TILES_DEV), widths.reshape(devices, TILES_DEV))

    def step(carry, block):
        decoded_rows, grad_in, grad_mid = decode_tiles(block[0], block[1], block[2], block[3], block[4], w_in, w_mid)
        return ((carry[0] + grad_in, carry[1] + grad_mid), decoded_rows)
    start = (jnp.zeros((TAPS * Z, C), jnp.float32), jnp.zeros((TAPS * C, C), jnp.float32))
    totals, decoded_all = lax.scan(step, start, blocks)
    ids = bucket_ids.reshape(devices, TILES_DEV)
    onehot = (ids[:, :, None] == jnp.arange(N_BUCKET, dtype=jnp.int32)[None, None, :]).astype(jnp.int32)
    before = jnp.cumsum(onehot, axis=1) - onehot
    rank = lax.optimization_barrier(jnp.sum(before * onehot, axis=2)).astype(jnp.int32)
    device_ids = jnp.arange(devices, dtype=jnp.int32)[:, None]
    group = device_ids // N_BUCKET
    source = device_ids % N_BUCKET
    target = (((group * N_BUCKET + ids) * N_BUCKET + source) * CAP + rank).astype(jnp.int32)
    decoded = jnp.zeros((SLOTS, TF * TH * TW * C), jnp.bfloat16).at[target.reshape(-1)].set(decoded_all.reshape(devices * TILES_DEV, -1))
    factor = 1.0 / jnp.sqrt(jnp.float32(TILES * TF * TH * TW))
    return (decoded, (totals[0] * factor).reshape(-1), (totals[1] * factor).reshape(-1))
```

```python
import math

import jax
import jax.numpy as jnp
from jax import lax
from jax.experimental import pallas as pl
from jax.experimental.pallas import tpu as pltpu
from jax.sharding import PartitionSpec as P

Z = 16
C = 384
TAPS = 27
TF = 2
TH = 4
TW = 4
CAP = 2
EPS = 1e-06
BF = jnp.bfloat16
F32 = jnp.float32
MESH = pl.DeviceIdType.MESH
ORDERS = (("z", "x", "y"), ("x", "y", "z"), ("y", "z", "x"))
ROWS = 1296
PIECE = 96
GROWS = 80


def al(v, m):
    return pl.multiple_of(v, m)


def kernel(
    xs_ref, snd_ref, cot_ref, mask_ref, win_ref, wmid_ref,
    dec_ref, gin_ref, gmid_ref,
    w, we, rcv, xsp, xbf, xbp, hf, uef, ut, gyef, gyep, gua, ghs, df, gif, gib, rgi, gz, gzb, rz, gx, gxb, rx,
    gyv, gyb, ry, g, rc, s1, p1, fl1, fr1, s2f, s2, p2, fl2, fr2, s3, p3, fl3, fr3, ud, acc,
    w_sem, a_send, a_recv, c_send, c_recv, r_send, r_recv, i_send, i_recv,
):
    load = lax.axis_index("loader")
    q = lax.axis_index("bucket")
    z, c = load // 2, load % 2
    x, y = q // 4, q % 4
    pos = {"z": z, "x": x, "y": y}
    sib = (z * 2 + (1 - c), q)

    def dev(axis, v):
        if axis == "z":
            return (v * 2 + c, q)
        if axis == "x":
            return (load, v * 4 + y)
        return (load, x * 4 + v)

    def wcopy(i):
        part = pl.ds(i * 1152, 1152)
        return pltpu.make_async_copy(wmid_ref.at[part], w.at[part], w_sem.at[i])

    for i in range(9):
        wcopy(i).start()

    barrier = pltpu.get_barrier_semaphore()

    @pl.loop(1, 16)
    def _(d):
        pl.semaphore_signal(barrier, 1, device_id=(load, lax.rem(q + d, 16)), device_id_type=MESH)

    for d in range(1, 4):
        pl.semaphore_signal(barrier, 1, device_id=dev("z", lax.rem(z + d, 4)), device_id_type=MESH)
    pl.semaphore_signal(barrier, 1, device_id=sib, device_id_type=MESH)
    pl.semaphore_wait(barrier, 19)

    def acopy(d):
        to = lax.rem(q + d, 16)
        return pltpu.make_async_remote_copy(
            snd_ref.at[to], rcv.at[q], a_send.at[d], a_recv.at[d], device_id=(load, to), device_id_type=MESH)

    def afrom(d):
        src = lax.rem(q - d + 16, 16)
        return pltpu.make_async_remote_copy(
            snd_ref.at[src], rcv.at[src], a_send.at[d], a_recv.at[d], device_id=(load, src), device_id_type=MESH)

    @pl.loop(1, 16)
    def _(d):
        acopy(d).start()

    rcv[q] = snd_ref[q]

    we[...] = jnp.zeros_like(we)
    for a in range(3):
        for b in range(3):
            for cc in range(4):
                for e in range(3):
                    ci = cc + e - 1
                    if 0 <= ci < 4:
                        we[a * 256 + (b * 4 + ci) * 16 : a * 256 + (b * 4 + ci) * 16 + 16, cc * C : cc * C + C] = (
                            win_ref[(a * 9 + b * 3 + e) * 16 : (a * 9 + b * 3 + e) * 16 + 16, :])

    xsp[0:64, :] = jnp.zeros((64, 256), BF)
    xsp[64:128, :] = xs_ref[...].astype(BF)
    h = jnp.dot(xsp[0:64, :], we[0:256, :], preferred_element_type=F32)
    h += jnp.dot(xsp[32:96, :], we[256:512, :], preferred_element_type=F32)
    h += jnp.dot(xsp[64:128, :], we[512:768, :], preferred_element_type=F32)
    for fr in range(8):
        for cc in range(4):
            hf[(fr * 4 + cc) * 8 : (fr * 4 + cc) * 8 + 8, :] = h[fr * 8 : fr * 8 + 8, cc * C : cc * C + C]

    def act(hv):
        rr = lax.rsqrt(jnp.mean(hv * hv, axis=-1, keepdims=True) + EPS)
        gv = hv * rr
        sg = jax.nn.sigmoid(gv)
        return rr, gv, sg

    hv = hf[...]
    rr, gn, sg = act(hv)
    u = gn * sg
    uef[...] = jnp.zeros_like(uef)
    gyef[...] = jnp.zeros_like(gyef)
    uef[:, C : 2 * C] = u
    cot = cot_ref[...].astype(F32)
    for p in range(32):
        gyef[p * 8 : p * 8 + 8, C : 2 * C] = jnp.where(
            mask_ref[:, p : p + 1] > 0, cot[:, p * C : p * C + C], 0.0)
    for fr in range(8):
        lo, hi = slice(fr * 32, fr * 32 + 24), slice(fr * 32 + 8, fr * 32 + 32)
        uef[hi, 0:C] = uef[lo, C : 2 * C]
        uef[lo, 2 * C : 3 * C] = uef[hi, C : 2 * C]
        gyef[lo, 0:C] = gyef[hi, C : 2 * C]
        gyef[hi, 2 * C : 3 * C] = gyef[lo, C : 2 * C]
    ut[...] = uef[...].T.astype(BF)
    gyep[...] = jnp.zeros_like(gyep)
    for f in range(2):
        gyep[(f * 6 + 1) * 32 : (f * 6 + 5) * 32, :] = gyef[f * 128 : f * 128 + 128, :].astype(BF)

    def ccopy(zz):
        return pltpu.make_async_remote_copy(
            g.at[pl.ds(al((zz * 2 + 1 - c) * ROWS, 16), ROWS)], rc.at[zz], c_send.at[zz], c_recv.at[zz],
            device_id=sib, device_id_type=MESH)

    def shifted(i, lanes):
        a, b = i // 3, i % 3
        o0 = al(((2 - a) * 6 + 2 - b) * 32, 32)
        o1 = al(((3 - a) * 6 + 2 - b) * 32, 32)
        return jnp.concatenate([gyep[pl.ds(o0, 128), lanes], gyep[pl.ds(o1, 128), lanes]], axis=0)

    @pl.loop(0, 9)
    def _(i):
        rhs = shifted(i, slice(C, 2 * C))
        g[pl.ds(al(i * 1152, 16), 1152), :] = jnp.dot(ut[...], rhs, preferred_element_type=F32).astype(BF)
        ready = i - 1

        @pl.when((i >= 1) & (lax.rem(ready + 2, 2) != c))
        def _():
            ccopy(ready // 2).start()

    def place(j, zz, xx, yy):
        at = {"z": zz, "x": xx, "y": yy}
        i1, i2, i3 = (at[n] for n in ORDERS[j])
        return j * 64 + i1 * 16 + i2 * 4 + i3

    for zz in range(4):
        ccopy(zz).wait_recv()

        @pl.loop(0, 16)
        def _(k):
            own = al((zz * 2 + c) * ROWS + k * 80, 16)
            other = al(k * 80, 16)
            for j in range(3):
                lanes = slice(j * 128, j * 128 + 128)
                s1[place(j, zz, k // 4, k % 4)] = (
                    g[pl.ds(own, PIECE), lanes].astype(F32) + rc[zz, pl.ds(other, PIECE), lanes].astype(F32)).astype(BF)

    def half1(j, t, h):
        return s1.at[pl.ds(j * 64 + t * 16 + h * 8, 8)]

    def half2(j, t, h):
        return s2.at[pl.ds(j * 16 + t * 4 + h * 2, 2)]

    def half3(j, t, h):
        return s3.at[j * 4 + t, h * 48 : h * 48 + 48]

    def from1(ref, j, h):
        return ref.at[pl.ds(j * 16 + h * 8, 8)]

    def from2(ref, j, h):
        return ref.at[pl.ds(j * 4 + h * 2, 2)]

    def from3(ref, j, h):
        return ref.at[j, h * 48 : h * 48 + 48]

    stages = ((half1, p1, fl1, fr1, from1), (half2, p2, fl2, fr2, from2), (half3, p3, fl3, fr3, from3))

    def ring(j, st, n):
        half, part, fl, fr, into = stages[st]
        axis = ORDERS[j][st]
        me = pos[axis]
        right, left, far = lax.rem(me + 1, 4), lax.rem(me + 3, 4), lax.rem(me + 2, 4)
        src, to, dst = (
            (half(j, far, 0), right, part.at[j * 2]),
            (half(j, far, 1), left, part.at[j * 2 + 1]),
            (half(j, right, 1), right, into(fl, j, 1)),
            (half(j, left, 0), left, into(fr, j, 0)),
            (half(j, right, 0), right, into(fl, j, 0)),
            (half(j, left, 1), left, into(fr, j, 1)),
        )[n]
        k = (j * 3 + st) * 6 + n
        return pltpu.make_async_remote_copy(
            src, dst, r_send.at[k], r_recv.at[k], device_id=dev(axis, to), device_id_type=MESH)

    def begin(st):
        for n in range(4):
            for j in range(3):
                ring(j, st, n).start()

    def relay(st):
        half, part = stages[st][0], stages[st][1]
        for n in range(2):
            for j in range(3):
                me = pos[ORDERS[j][st]]
                ring(j, st, n).wait_recv()
                ref = half(j, lax.rem(me + (1 if n == 0 else 3), 4), n)
                ref[...] = (ref[...].astype(F32) + part[j * 2 + n].astype(F32)).astype(ref.dtype)
                ring(j, st, 4 + n).start()

    def arrived(st):
        for j in range(3):
            for n in range(2, 6):
                ring(j, st, n).wait_recv()

    def finish1():
        arrived(0)
        for j in range(3):

            @pl.loop(0, 16)
            def _(k):
                at = {ORDERS[j][0]: pos[ORDERS[j][0]], ORDERS[j][1]: k // 4, ORDERS[j][2]: k % 4}
                off = (at["x"] * 4 + at["y"]) * 80
                lanes = slice(j * 128, j * 128 + 128)
                total = (
                    g[pl.ds(al((at["z"] * 2 + c) * ROWS + off, 16), PIECE), lanes].astype(F32)
                    + rc[at["z"], pl.ds(al(off, 16), PIECE), lanes].astype(F32)
                    + fl1[j * 16 + k].astype(F32) + fr1[j * 16 + k].astype(F32))
                s2f[j * 16 + k] = total
                s2[j * 16 + k] = total.astype(BF)

    def finish2():
        arrived(1)
        for j in range(3):
            me = pos[ORDERS[j][1]]
            for k in range(4):
                s3[j * 4 + k] = s2f[j * 16 + me * 4 + k] + fl2[j * 4 + k].astype(F32) + fr2[j * 4 + k].astype(F32)

    def finish3():
        arrived(2)
        for j in range(3):
            gmid_ref[:, j * 128 : j * 128 + 128] = s3[j * 4 + pos[ORDERS[j][2]]] + fl3[j] + fr3[j]

    begin(0)

    for i in range(9):
        wcopy(i).wait()
    gua[...] = jnp.zeros_like(gua)

    @pl.loop(0, 9)
    def _(i):
        total = gua[...]
        for e in range(3):
            lhs = shifted(i, slice(e * C, e * C + C))
            wk = w[pl.ds(al(i * 1152 + e * C, 16), C), :]
            total += lax.dot_general(lhs, wk, (((1,), (1,)), ((), ())), preferred_element_type=F32)
        gua[...] = total

    rr, gn, sg = act(hf[...])
    gv = gua[...] * sg * (1.0 + gn * (1.0 - sg))
    gh = gyef[:, C : 2 * C] + rr * (gv - gn * jnp.mean(gv * gn, axis=-1, keepdims=True))
    hf[...] = gh
    ghs[...] = jnp.zeros_like(ghs)
    for cc in range(4):
        ghs[0:64, cc * C : cc * C + C] = jnp.concatenate(
            [hf[(fr * 4 + cc) * 8 : (fr * 4 + cc) * 8 + 8, :] for fr in range(8)], axis=0).astype(BF)
    xst = xs_ref[...].T.astype(BF)
    gif[...] = jnp.zeros_like(gif)
    for a in range(3):
        df[...] = jnp.dot(xst, ghs[(2 - a) * 32 : (2 - a) * 32 + 64, :], preferred_element_type=F32)
        for b in range(3):
            for e in range(3):
                total = jnp.zeros((16, C), F32)
                for cc in range(4):
                    ci = cc + e - 1
                    if 0 <= ci < 4:
                        total += df[(b * 4 + ci) * 16 : (b * 4 + ci) * 16 + 16, cc * C : cc * C + C]
                gif[(a * 9 + b * 3 + e) * 16 : (a * 9 + b * 3 + e) * 16 + 16, :] = total
    for blk in range(8):
        at = 16 * ((27 * blk) // 8)
        gib[blk % 2, blk // 2] = gif[at : at + GROWS, :].astype(BF)

    def icore():
        return pltpu.make_async_remote_copy(
            gib.at[1 - c], rgi, i_send.at[0], i_recv.at[0], device_id=sib, device_id_type=MESH)

    base = load * 54 - 16 * ((27 * load) // 8)

    def xstart(v):
        return al(16 * ((2 * base + 27 * v) // 32), 16)

    def ipeer(axis, d):
        v = lax.rem(pos[axis] + d, 4)
        src, dst, k = {
            "z": (gzb.at[v], rz.at[d - 1], 0),
            "x": (gxb.at[pl.ds(xstart(v), 32)], rx.at[d - 1], 3),
            "y": (gyb, ry.at[d - 1], 6),
        }[axis]
        return pltpu.make_async_remote_copy(
            src, dst, i_send.at[k + d], i_recv.at[k + d], device_id=dev(axis, v), device_id_type=MESH)

    def in_z():
        icore().wait_recv()
        for zz in range(4):
            at = al(16 * ((27 * (zz * 2 + c)) // 8), 16)
            total = gif[pl.ds(at, GROWS), :] + rgi[zz].astype(F32)
            gz[zz] = total
            gzb[zz] = total.astype(BF)
        for d in range(1, 4):
            ipeer("z", d).start()

    def in_x():
        for d in range(1, 4):
            ipeer("z", d).wait_recv()
        total = gz[z] + rz[0].astype(F32) + rz[1].astype(F32) + rz[2].astype(F32)
        gx[...] = total
        gxb[...] = total.astype(BF)
        for d in range(1, 4):
            ipeer("x", d).start()

    def in_y():
        for d in range(1, 4):
            ipeer("x", d).wait_recv()
        total = gx[pl.ds(xstart(x), 32), :] + rx[0].astype(F32) + rx[1].astype(F32) + rx[2].astype(F32)
        gyv[...] = total
        gyb[...] = total.astype(BF)
        for d in range(1, 4):
            ipeer("y", d).start()

    def in_end():
        for d in range(1, 4):
            ipeer("y", d).wait_recv()
        gin_ref[...] = gyv[...] + ry[0].astype(F32) + ry[1].astype(F32) + ry[2].astype(F32)

    icore().start()
    relay(0)

    @pl.loop(1, 16)
    def _(d):
        afrom(d).wait_recv()

    for fr in range(8):
        for j in range(2):
            for n in range(2):
                xbf[n, pl.ds(fr * 32 + j, 16, stride=2), :] = rcv[:, fr, j * 256 + n * 128 : j * 256 + n * 128 + 128]
    xbp[0:256, :] = jnp.zeros((256, 256), BF)
    xbp[256:512, 0:128] = xbf[0].astype(BF)
    xbp[256:512, 128:256] = xbf[1].astype(BF)
    ud[...] = jnp.zeros_like(ud)
    for f in range(2):
        hd = jnp.dot(xbp[f * 128 : f * 128 + 128, :], we[0:256, :], preferred_element_type=F32)
        hd += jnp.dot(xbp[f * 128 + 128 : f * 128 + 256, :], we[256:512, :], preferred_element_type=F32)
        hd += jnp.dot(xbp[f * 128 + 256 : f * 128 + 384, :], we[512:768, :], preferred_element_type=F32)
        for cc in range(4):
            hc = hd[:, cc * C : cc * C + C]
            _, gc, sc = act(hc)
            uc = (gc * sc).astype(BF)
            for r in range(4):
                rows = slice(r * 32, r * 32 + 32)
                acc[((f * 4 + r) * 4 + cc) * 32 : ((f * 4 + r) * 4 + cc) * 32 + 32, :] = hc[rows]
                to = ((f + 2) * 6 + r + 1) * 128 + cc * 32
                for e in range(3):
                    if 0 <= cc - e + 1 < 4:
                        ud[to + (1 - e) * 32 : to + (1 - e) * 32 + 32, e * C : e * C + C] = uc[rows]

    def second():
        finish1()
        begin(1)

    def third():
        finish2()
        begin(2)

    events = {
        0: in_z, 3: in_x, 6: in_y, 9: in_end,
        10: second, 12: lambda: relay(1), 14: third, 15: lambda: relay(2),
    }

    @pl.loop(0, 18)
    def _(s):
        f, i = s // 9, lax.rem(s, 9)
        a, b = i // 3, lax.rem(i, 3)
        lhs = ud[pl.ds(al(((f + a) * 6 + b) * 128, 128), 512), :]
        rows = pl.ds(al(f * 512, 512), 512)
        acc[rows, :] += jnp.dot(lhs, w[pl.ds(al(i * 1152, 16), 1152), :], preferred_element_type=F32)
        for at, event in events.items():
            pl.when(s == at)(event)

    for fr in range(8):
        for cc in range(4):
            p = fr * 4 + cc
            m = xbf[1, fr * 32 : fr * 32 + 32, 64 + cc : 65 + cc]
            dec_ref[:, p * C : p * C + C] = (acc[p * 32 : p * 32 + 32, :] * m).astype(BF)
    finish3()

    @pl.loop(1, 16)
    def _(d):
        acopy(d).wait_send()

    for zz in range(4):
        ccopy(zz).wait_send()
    for st in range(3):
        for j in range(3):
            for n in range(6):
                ring(j, st, n).wait_send()
    icore().wait_send()
    for axis in ("z", "x", "y"):
        for d in range(1, 4):
            ipeer(axis, d).wait_send()


def tile_mask(frames, heights, widths):
    fpos = jnp.arange(TF)[None, :, None, None]
    rpos = jnp.arange(TH)[None, None, :, None]
    cpos = jnp.arange(TW)[None, None, None, :]
    inside = (
        (fpos < frames[:, None, None, None])
        & (rpos < heights[:, None, None, None])
        & (cpos < widths[:, None, None, None])
    )
    return inside.astype(F32)


def shards(latents, cotangent, frames, heights, widths, bucket_ids, w_in, w_mid):
    owners = lax.axis_size("bucket")
    count = latents.shape[0]
    tiles_total = count * lax.axis_size("loader") * owners
    mask = tile_mask(frames, heights, widths)
    xm = latents.reshape(count, TF, TH, TW, Z).astype(F32) * mask[..., None]
    xm = jnp.pad(xm.reshape(count, TF, TH, TW * Z), ((0, 0), (0, 0), (1, 1), (0, 0)))
    xb = jnp.concatenate(
        [xm[:, :, 0:4], xm[:, :, 1:5], xm[:, :, 2:6], mask, jnp.zeros((count, TF, TH, 60), F32)], axis=-1
    ).reshape(count, 8, 256)
    same = bucket_ids[:, None] == bucket_ids[None, :]
    rank = jnp.sum(jnp.tril(same, -1).astype(jnp.int32), axis=1)
    slot = bucket_ids * CAP + rank
    placer = (slot[None, :] == jnp.arange(owners * CAP, dtype=jnp.int32)[:, None]).astype(F32)
    snd = jnp.dot(placer, xb.reshape(count, 2048), preferred_element_type=F32)
    snd = snd.reshape(owners, CAP, 8, 256).transpose(0, 2, 1, 3).reshape(owners, 8, 512)
    xs = xb.transpose(1, 0, 2).reshape(64, 256)

    v = pltpu.VMEM
    dma = pltpu.SemaphoreType.DMA
    vm = pl.BlockSpec(memory_space=pltpu.VMEM)
    dec, gin, gmid = pl.pallas_call(
        kernel,
        out_shape=(
            jax.ShapeDtypeStruct((32, 12288), BF),
            jax.ShapeDtypeStruct((32, C), F32),
            jax.ShapeDtypeStruct((PIECE, C), F32),
        ),
        in_specs=[vm, vm, vm, vm, vm, pl.BlockSpec(memory_space=pl.ANY)],
        out_specs=(vm, vm, vm),
        scratch_shapes=[
            v((10368, C), BF), v((768, 1536), BF), v((16, 8, 512), F32), v((128, 256), BF), v((2, 256, 128), F32),
            v((512, 256), BF), v((256, C), F32), v((256, 1152), F32), v((1152, 256), BF), v((256, 1152), F32),
            v((768, 1152), BF), v((256, C), F32), v((128, 1536), BF), v((256, 1536), F32), v((448, C), F32),
            v((2, 4, GROWS, C), BF), v((4, GROWS, C), BF), v((4, GROWS, C), F32), v((4, GROWS, C), BF),
            v((3, GROWS, C), BF), v((GROWS, C), F32), v((GROWS, C), BF), v((3, 32, C), BF),
            v((32, C), F32), v((32, C), BF), v((3, 32, C), BF), v((10368, C), BF), v((4, ROWS, C), BF),
            v((192, PIECE, 128), BF), v((6, 8, PIECE, 128), BF), v((48, PIECE, 128), BF), v((48, PIECE, 128), BF),
            v((48, PIECE, 128), F32), v((48, PIECE, 128), BF), v((6, 2, PIECE, 128), BF), v((12, PIECE, 128), BF),
            v((12, PIECE, 128), BF), v((12, PIECE, 128), F32), v((6, 48, 128), F32), v((3, PIECE, 128), F32),
            v((3, PIECE, 128), F32), v((3072, 1152), BF), v((1024, C), F32),
            dma((9,)), dma((16,)), dma((16,)), dma((4,)), dma((4,)), dma((54,)), dma((54,)), dma((10,)), dma((10,)),
        ],
        compiler_params=pltpu.CompilerParams(
            collective_id=0, has_side_effects=True, vmem_limit_bytes=62 * 1024 * 1024),
    )(xs, snd, cotangent, mask.reshape(count, 32), w_in, w_mid)

    factor = 1.0 / math.sqrt(tiles_total * TF * TH * TW)
    load = lax.axis_index("loader")
    q = lax.axis_index("bucket")
    base = load * 54 - 16 * ((27 * load) // 8)
    start = 16 * ((2 * base + 27 * (q // 4)) // 32)
    grad_in = lax.dynamic_slice(gin.reshape(-1), (384 * (base - start) + 1296 * q,), (1296,)) * factor
    grad_mid = lax.dynamic_slice(gmid, (q, 0), (81, C)).reshape(-1) * factor
    return (dec, grad_in, grad_mid)


def solution(mesh):
    return jax.shard_map(
        shards,
        mesh=mesh,
        in_specs=(
            P(("loader", "bucket"), None),
            P(("loader", "bucket"), None),
            P(("loader", "bucket")),
            P(("loader", "bucket")),
            P(("loader", "bucket")),
            P(("loader", "bucket")),
            P(),
            P(),
        ),
        out_specs=(P(("loader", "bucket"), None), P(("loader", "bucket")), P(("loader", "bucket"))),
        check_vma=False,
    )
```

```python
import math

import jax
import jax.numpy as jnp
from jax import lax
from jax.experimental import pallas as pl
from jax.experimental.pallas import tpu as pltpu
from jax.sharding import PartitionSpec as P

Z = 16
C = 384
TAPS = 27
TF = 2
TH = 4
TW = 4
CAP = 2
EPS = 1e-06
BF = jnp.bfloat16
F32 = jnp.float32
MESH = pl.DeviceIdType.MESH
ORDERS = (("z", "x", "y"), ("x", "y", "z"), ("y", "z", "x"))
ROWS = 1296
FACTOR = 1.0 / math.sqrt(1024 * TF * TH * TW)
PIECE = 96
GROWS = 80


def al(v, m):
    return pl.multiple_of(v, m)


def kernel(
    ids_ref, fra_ref, hei_ref, wid_ref, lat_ref, cot_ref, win_ref, wmid_ref,
    dec_ref, gin_ref, gmid_ref,
    w, we, snd, rcv, xsf, xsp, xbf, xbp, hf, ub, gb, ru, rg, uef, ut, gyef, gyep, gyes, ghs, df, gif, gib, rgi, gz, gzb,
    rz, gx, gxb, rx, gyv, gyb, ry, g, s1, pa0, pb0, fl0, fr0, pa1, pb1, fl1, fr1, pa2, pb2, fl2, fr2, s2f, s2, f2,
    s3, f3, fm, fg, ud, acc,
    w_sem, a_send, a_recv, c_send, c_recv, r_send, r_recv, d_send, d_recv, i_send, i_recv,
):
    load = lax.axis_index("loader")
    q = lax.axis_index("bucket")
    z, c = load // 2, load % 2
    x, y = q // 4, q % 4
    pos = {"z": z, "x": x, "y": y}
    sib = (z * 2 + (1 - c), q)

    def dev(axis, v):
        if axis == "z":
            return (v * 2 + c, q)
        if axis == "x":
            return (load, v * 4 + y)
        return (load, x * 4 + v)

    def wcopy(i):
        part = pl.ds(i * 1152, 1152)
        return pltpu.make_async_copy(wmid_ref.at[part], w.at[part], w_sem.at[i])

    for i in range(9):
        wcopy(i).start()

    barrier = pltpu.get_barrier_semaphore()

    @pl.loop(1, 16)
    def _(d):
        pl.semaphore_signal(barrier, 1, device_id=(load, lax.rem(q + d, 16)), device_id_type=MESH)

    for d in range(1, 4):
        pl.semaphore_signal(barrier, 1, device_id=dev("z", lax.rem(z + d, 4)), device_id_type=MESH)
    pl.semaphore_signal(barrier, 1, device_id=sib, device_id_type=MESH)

    def iota(shape, dim):
        return lax.broadcasted_iota(jnp.int32, shape, dim)

    def column(ref):
        at, out = iota((8, 1), 0), jnp.zeros((8, 1), jnp.int32)
        for t in range(8):
            out = jnp.where(at == t, ref[t], out)
        return out

    fra, hei, wid = column(fra_ref), column(hei_ref), column(wid_ref)
    lane = iota((8, 512), 1)
    inside = (lane // 256 < fra) & ((lane // 64) % 4 < hei) & ((lane // 16) % 4 < wid)
    xm = jnp.where(inside, lat_ref[...].astype(F32), 0.0)
    edge = jnp.zeros((8, 128), F32)
    xm = jnp.concatenate([edge, xm, edge], axis=1)
    xh = pltpu.roll(xm, 704, 1)
    lane = iota((8, 256), 1)
    for fr in range(8):
        f, r = fr // 4, fr % 4
        win = xm[:, 64 * fr + 64 : 64 * fr + 320] if fr % 2 else xh[:, 64 * fr : 64 * fr + 256]
        keep = lane < 192
        if r == 0:
            keep = keep & (lane >= 64)
        if r == 3:
            keep = keep & (lane < 128)
        ones = (lane >= 192) & (lane - 192 < wid) & (f < fra) & (r < hei)
        xsf[fr * 8 : fr * 8 + 8, :] = jnp.where(keep, win, jnp.where(ones, 1.0, 0.0))
    xs = xsf[...].astype(BF)

    ids = [ids_ref[t] for t in range(8)]
    lane, row = iota((1, 64), 1), iota((256, 64), 0)
    slots = jnp.zeros((1, 64), jnp.int32)
    for t in range(8):
        rank = jnp.int32(0)
        for before in range(t):
            rank += jnp.where(ids[before] == ids[t], 1, 0)
        slots = jnp.where(lane % 8 == t, ids[t] * CAP + rank, slots)
    pick = (row // 16 * 2 + row % 2 == slots) & ((row // 2) % 8 == lane // 8)
    snd[...] = jnp.dot(jnp.where(pick, 1.0, 0.0).astype(BF), xs, preferred_element_type=F32).astype(BF)

    def acopy(d):
        to = lax.rem(q + d, 16)
        return pltpu.make_async_remote_copy(
            snd.at[pl.ds(al(to * 16, 16), 16)], rcv.at[pl.ds(al(q * 16, 16), 16)],
            a_send.at[d], a_recv.at[d], device_id=(load, to), device_id_type=MESH)

    def afrom(d):
        src = lax.rem(q - d + 16, 16)
        rows = pl.ds(al(src * 16, 16), 16)
        return pltpu.make_async_remote_copy(
            snd.at[rows], rcv.at[rows], a_send.at[d], a_recv.at[d], device_id=(load, src), device_id_type=MESH)

    we[...] = jnp.zeros_like(we)
    for a in range(3):
        for b in range(3):
            for cc in range(4):
                for e in range(3):
                    ci = cc + e - 1
                    if 0 <= ci < 4:
                        we[a * 256 + (b * 4 + ci) * 16 : a * 256 + (b * 4 + ci) * 16 + 16, cc * C : cc * C + C] = (
                            win_ref[(a * 9 + b * 3 + e) * 16 : (a * 9 + b * 3 + e) * 16 + 16, :])

    xsp[0:64, :] = jnp.zeros((64, 256), BF)
    xsp[64:128, :] = xs
    h = jnp.dot(xsp[0:64, :], we[0:256, :], preferred_element_type=F32)
    h += jnp.dot(xsp[32:96, :], we[256:512, :], preferred_element_type=F32)
    h += jnp.dot(xsp[64:128, :], we[512:768, :], preferred_element_type=F32)
    for fr in range(8):
        for cc in range(4):
            hf[(fr * 4 + cc) * 8 : (fr * 4 + cc) * 8 + 8, :] = h[fr * 8 : fr * 8 + 8, cc * C : cc * C + C]

    def act(hv):
        rr = lax.rsqrt(jnp.mean(hv * hv, axis=-1, keepdims=True) + EPS)
        gv = hv * rr
        sg = jax.nn.sigmoid(gv)
        return rr, gv, sg

    rr, gn, sg = act(hf[...])
    u = gn * sg
    ub[...] = u.astype(BF)
    cot = cot_ref[...].astype(F32)
    for p in range(32):
        inside = (p // 16 < fra) & ((p // 4) % 4 < hei) & (p % 4 < wid)
        gyef[p * 8 : p * 8 + 8, C : 2 * C] = jnp.where(inside, cot[:, p * C : p * C + C], 0.0)
    gb[...] = gyef[:, C : 2 * C].astype(BF)

    def swap(n):
        src, dst = ((ub, ru), (gb, rg))[n]
        return pltpu.make_async_remote_copy(
            src, dst, c_send.at[n], c_recv.at[n], device_id=sib, device_id_type=MESH)

    pl.semaphore_wait(barrier, 19)
    swap(0).start()
    swap(1).start()

    @pl.loop(1, 16)
    def _(d):
        acopy(d).start()

    own = pl.ds(al(q * 16, 16), 16)
    rcv[own, :] = snd[own, :]

    def spread_u(uv, lanes):
        uef[:, C : 2 * C] = uv
        for fr in range(8):
            lo, hi = slice(fr * 32, fr * 32 + 24), slice(fr * 32 + 8, fr * 32 + 32)
            uef[hi, 0:C] = uef[lo, C : 2 * C]
            uef[lo, 2 * C : 3 * C] = uef[hi, C : 2 * C]
        ut[:, lanes] = uef[...].T.astype(BF)

    uef[...] = jnp.zeros_like(uef)
    spread_u(u, slice(0, 256))
    for fr in range(8):
        lo, hi = slice(fr * 32, fr * 32 + 24), slice(fr * 32 + 8, fr * 32 + 32)
        gyef[lo, 0:C] = gyef[hi, C : 2 * C]
        gyef[fr * 32 + 24 : fr * 32 + 32, 0:C] = jnp.zeros((8, C), F32)
        gyef[hi, 2 * C : 3 * C] = gyef[lo, C : 2 * C]
        gyef[fr * 32 : fr * 32 + 8, 2 * C : 3 * C] = jnp.zeros((8, C), F32)
    gyep[...] = jnp.zeros_like(gyep)
    gyes[...] = jnp.zeros_like(gyes)
    for f in range(2):
        gyep[(f * 6 + 1) * 32 : (f * 6 + 5) * 32, :] = gyef[f * 128 : f * 128 + 128, :].astype(BF)
    swap(0).wait_recv()
    spread_u(ru[...].astype(F32), slice(256, 512))
    swap(1).wait_recv()
    for f in range(2):
        gyes[(f * 6 + 1) * 32 : (f * 6 + 5) * 32, :] = rg[f * 128 : f * 128 + 128, :]

    def shifted(ref, i, lanes):
        a, b = i // 3, i % 3
        o0, o1 = ((2 - a) * 6 + 2 - b) * 32, ((3 - a) * 6 + 2 - b) * 32
        return jnp.concatenate([ref[o0 : o0 + 128, lanes], ref[o1 : o1 + 128, lanes]], axis=0)

    def weight_grad(zz, core):
        first = (zz * 2 + core) * ROWS
        at = first
        while at < first + ROWS:
            i = at // 1152
            lo, hi = at - i * 1152, min(1152, first + ROWS - i * 1152)
            rhs = jnp.concatenate(
                [shifted(gyep, i, slice(C, 2 * C)), shifted(gyes, i, slice(0, C))], axis=0)
            out = jnp.dot(ut[lo:hi, :], rhs, preferred_element_type=F32).astype(BF)
            for j in range(3):
                g[j, zz, at - first : at - first + hi - lo, :] = out[:, j * 128 : j * 128 + 128]
            at += hi - lo

    CUT = 656

    def own1(j, t, h):
        if j == 0:
            return g.at[0, t, CUT * h : (CUT, ROWS)[h]]
        if j == 1:
            return g.at[1, 2 * h : 2 * h + 2, pl.ds(al(320 * t, 16), 336)]
        return s1.at[pl.ds(t * 16 + h * 8, 8)]

    def into(j, side, h):
        ref = ((fl0, fr0), (fl1, fr1), (fl2, fr2))[j][side]
        return ref.at[((0, CUT), (0, 2), (0, 8))[j][h] : ((CUT, ROWS), (2, 4), (8, 16))[j][h]]

    parts = ((pa0, pb0), (pa1, pb1), (pa2, pb2))

    def target(j, n):
        return lax.rem(pos[ORDERS[j][0]] + (2, 2, 1, 3, 1, 3)[n], 4)

    def ring(j, n):
        axis = ORDERS[j][0]
        src, side, dst = (
            (own1(j, target(j, 0), 0), 1, parts[j][0]),
            (own1(j, target(j, 1), 1), 3, parts[j][1]),
            (own1(j, target(j, 2), 1), 1, into(j, 0, 1)),
            (own1(j, target(j, 3), 0), 3, into(j, 1, 0)),
            (parts[j][0], 1, into(j, 0, 0)),
            (parts[j][1], 3, into(j, 1, 1)),
        )[n]
        k = j * 6 + n
        return pltpu.make_async_remote_copy(
            src, dst, r_send.at[k], r_recv.at[k], device_id=dev(axis, lax.rem(pos[axis] + side, 4)),
            device_id_type=MESH)

    def relay():
        for n in range(2):
            for j in range(3):
                ring(j, n).wait_recv()
                ref = parts[j][n]
                ref[...] = ref[...] + own1(j, target(j, 4 + n), n)[...]
                ring(j, 4 + n).start()

    for group in range(2):
        for core in range(2):

            @pl.when(c == core)
            def _():
                weight_grad(group * 2, core)
                weight_grad(group * 2 + 1, core)

        @pl.loop(0, 32)
        def _(k):
            zz, shard = group * 2 + k // 16, lax.rem(k, 16)
            s1[lax.rem(shard, 4) * 16 + zz * 4 + shard // 4] = g[2, zz, pl.ds(al(shard * 80, 16), PIECE), :]

        for n in (0, 3) if group == 0 else (1, 2):
            for j in (2, 1):
                ring(j, n).start()
        for n in range(4):

            @pl.when(target(0, n) // 2 == group)
            def _():
                ring(0, n).start()

    def direct(j, st, d):
        axis = ORDERS[j][st]
        to = lax.rem(pos[axis] + d, 4)
        if st == 1:
            src, dst = s2.at[pl.ds(j * 16 + to * 4, 4)], f2.at[j * 3 + d - 1]
        else:
            src, dst = s3.at[j * 4 + to], f3.at[j * 3 + d - 1]
        k = (st - 1) * 9 + j * 3 + d - 1
        return pltpu.make_async_remote_copy(
            src, dst, d_send.at[k], d_recv.at[k], device_id=dev(axis, to), device_id_type=MESH)

    def second():
        for j in range(3):
            for n in range(2, 6):
                ring(j, n).wait_recv()

            @pl.loop(0, 16)
            def _(k):
                if j == 0:
                    rows = pl.ds(al(k * 80, 16), PIECE)
                    terms = g[0, z, rows, :], fl0[rows, :], fr0[rows, :]
                elif j == 1:
                    yy, zz = k // 4, lax.rem(k, 4)
                    rows = pl.ds(al(yy * 80, 16), PIECE)
                    terms = g[1, zz, pl.ds(al(x * 320 + yy * 80, 16), PIECE), :], fl1[zz, rows, :], fr1[zz, rows, :]
                else:
                    terms = s1[y * 16 + k], fl2[k], fr2[k]
                total = terms[0].astype(F32) + terms[1].astype(F32) + terms[2].astype(F32)
                s2f[j * 16 + k] = total
                s2[j * 16 + k] = total.astype(BF)

            for d in (2, 1, 3):
                direct(j, 1, d).start()

    def third():
        for j in range(3):
            for d in range(1, 4):
                direct(j, 1, d).wait_recv()
            for k in range(4):
                total = s2f[j * 16 + pos[ORDERS[j][1]] * 4 + k]
                for d in range(3):
                    total += f2[j * 3 + d, k].astype(F32)
                s3[j * 4 + k] = total
            for d in (2, 1, 3):
                direct(j, 2, d).start()

    def finish():
        for j in range(3):
            for d in range(1, 4):
                direct(j, 2, d).wait_recv()
            fm[j, 0:PIECE, :] = s3[j * 4 + pos[ORDERS[j][2]]] + f3[j * 3] + f3[j * 3 + 1] + f3[j * 3 + 2]
            fm[j, PIECE:, :] = jnp.zeros((8, 128), F32)
            gmid_ref[pl.ds(j, 88, stride=3), :] = fm[j, pl.ds(q, 88), :] * FACTOR


    for i in range(9):
        wcopy(i).wait()
    gu = jnp.zeros((256, C), F32)
    for i in range(9):
        for e in range(3):
            gu += lax.dot_general(
                shifted(gyep, i, slice(e * C, e * C + C)), w[i * 1152 + e * C : i * 1152 + e * C + C, :],
                (((1,), (1,)), ((), ())), preferred_element_type=F32)

    rr, gn, sg = act(hf[...])
    gv = gu * sg * (1.0 + gn * (1.0 - sg))
    gh = gyef[:, C : 2 * C] + rr * (gv - gn * jnp.mean(gv * gn, axis=-1, keepdims=True))
    hf[...] = gh
    ghs[...] = jnp.zeros_like(ghs)
    for cc in range(4):
        ghs[0:64, cc * C : cc * C + C] = jnp.concatenate(
            [hf[(fr * 4 + cc) * 8 : (fr * 4 + cc) * 8 + 8, :] for fr in range(8)], axis=0).astype(BF)
    xst = xsf[...].T.astype(BF)
    gif[...] = jnp.zeros_like(gif)
    for a in range(3):
        df[...] = jnp.dot(xst, ghs[(2 - a) * 32 : (2 - a) * 32 + 64, :], preferred_element_type=F32)
        for b in range(3):
            for e in range(3):
                total = jnp.zeros((16, C), F32)
                for cc in range(4):
                    ci = cc + e - 1
                    if 0 <= ci < 4:
                        total += df[(b * 4 + ci) * 16 : (b * 4 + ci) * 16 + 16, cc * C : cc * C + C]
                gif[(a * 9 + b * 3 + e) * 16 : (a * 9 + b * 3 + e) * 16 + 16, :] = total
    for blk in range(8):
        at = 16 * ((27 * blk) // 8)
        gib[blk % 2, blk // 2] = gif[at : at + GROWS, :].astype(BF)

    def icore():
        return pltpu.make_async_remote_copy(
            gib.at[1 - c], rgi, i_send.at[0], i_recv.at[0], device_id=sib, device_id_type=MESH)

    base = load * 54 - 16 * ((27 * load) // 8)

    def xstart(v):
        return al(16 * ((2 * base + 27 * v) // 32), 16)

    def ipeer(axis, d):
        v = lax.rem(pos[axis] + d, 4)
        src, dst, k = {
            "z": (gzb.at[v], rz.at[d - 1], 0),
            "x": (gxb.at[pl.ds(xstart(v), 32)], rx.at[d - 1], 3),
            "y": (gyb, ry.at[d - 1], 6),
        }[axis]
        return pltpu.make_async_remote_copy(
            src, dst, i_send.at[k + d], i_recv.at[k + d], device_id=dev(axis, v), device_id_type=MESH)

    def in_z():
        icore().wait_recv()
        for zz in range(4):
            at = al(16 * ((27 * (zz * 2 + c)) // 8), 16)
            total = gif[pl.ds(at, GROWS), :] + rgi[zz].astype(F32)
            gz[zz] = total
            gzb[zz] = total.astype(BF)
        for d in range(1, 4):
            ipeer("z", d).start()

    def in_x():
        for d in range(1, 4):
            ipeer("z", d).wait_recv()
        total = gz[z] + rz[0].astype(F32) + rz[1].astype(F32) + rz[2].astype(F32)
        gx[...] = total
        gxb[...] = total.astype(BF)
        for d in range(1, 4):
            ipeer("x", d).start()

    def in_y():
        for d in range(1, 4):
            ipeer("x", d).wait_recv()
        total = gx[pl.ds(xstart(x), 32), :] + rx[0].astype(F32) + rx[1].astype(F32) + rx[2].astype(F32)
        gyv[...] = total
        gyb[...] = total.astype(BF)
        for d in range(1, 4):
            ipeer("y", d).start()

    def in_end():
        for d in range(1, 4):
            ipeer("y", d).wait_recv()
        total = gyv[...] + ry[0].astype(F32) + ry[1].astype(F32) + ry[2].astype(F32)
        fg[96:, :] = jnp.zeros((8, 128), F32)
        for j in range(3):
            fg[pl.ds(j, 32, stride=3), :] = total[:, j * 128 : j * 128 + 128]
        first = 384 * (base - 16 * ((2 * base + 27 * x) // 32)) + 1296 * q
        at, lo = first // 128, lax.rem(first, 128)
        shift = lax.rem(128 - lo, 128)
        head = pltpu.roll(fg[pl.ds(at, 16), :], shift, 1)
        tail = pltpu.roll(fg[pl.ds(at + 1, 16), :], shift, 1)
        gin_ref[...] = jnp.where(iota((16, 128), 1) < 128 - lo, head, tail) * FACTOR

    icore().start()
    relay()
    in_z()

    @pl.loop(1, 16)
    def _(d):
        afrom(d).wait_recv()

    dst, src = iota((256, 256), 0), iota((256, 256), 1)
    order = (dst // 32 == (src // 2) % 8) & ((dst // 2) % 16 == src // 16) & (dst % 2 == src % 2)
    xbf[...] = jnp.dot(jnp.where(order, 1.0, 0.0).astype(BF), rcv[...], preferred_element_type=F32)
    xbp[0:256, :] = jnp.zeros((256, 256), BF)
    xbp[256:512, :] = xbf[...].astype(BF)
    ud[...] = jnp.zeros_like(ud)
    for f in range(2):
        hd = jnp.dot(xbp[f * 128 : f * 128 + 128, :], we[0:256, :], preferred_element_type=F32)
        hd += jnp.dot(xbp[f * 128 + 128 : f * 128 + 256, :], we[256:512, :], preferred_element_type=F32)
        hd += jnp.dot(xbp[f * 128 + 256 : f * 128 + 384, :], we[512:768, :], preferred_element_type=F32)
        for cc in range(4):
            hc = hd[:, cc * C : cc * C + C]
            _, gc, sc = act(hc)
            uc = (gc * sc).astype(BF)
            for r in range(4):
                rows = slice(r * 32, r * 32 + 32)
                acc[((f * 4 + r) * 4 + cc) * 32 : ((f * 4 + r) * 4 + cc) * 32 + 32, :] = hc[rows]
                to = (f + 2) * 512 + r * 128 + cc * 32
                for e in range(3):
                    if 0 <= cc - e + 1 < 4:
                        ud[to + (1 - e) * 32 : to + (1 - e) * 32 + 32, e * C : e * C + C] = uc[rows]

    def decode(a, f):
        taps = jnp.concatenate([w[(a * 3 + b) * 1152 : (a * 3 + b) * 1152 + 1152, :] for b in range(3)], axis=1)
        out = jnp.dot(ud[(f + a) * 512 : (f + a) * 512 + 512, :], taps, preferred_element_type=F32)
        top = f * 512
        acc[top + 128 : top + 512, :] += out[0:384, 0:C]
        acc[top : top + 512, :] += out[:, C : 2 * C]
        acc[top : top + 384, :] += out[128:512, 2 * C :]

    decode(0, 0)
    decode(0, 1)
    second()
    in_x()
    decode(1, 0)
    decode(1, 1)
    third()
    in_y()
    decode(2, 0)
    decode(2, 1)
    for fr in range(8):
        for cc in range(4):
            p = fr * 4 + cc
            m = xbf[fr * 32 : fr * 32 + 32, 192 + cc : 193 + cc]
            dec_ref[:, p * C : p * C + C] = (acc[p * 32 : p * 32 + 32, :] * m).astype(BF)
    finish()
    in_end()

    @pl.loop(1, 16)
    def _(d):
        acopy(d).wait_send()

    swap(0).wait_send()
    swap(1).wait_send()
    for j in range(3):
        for n in range(6):
            ring(j, n).wait_send()
        for d in range(1, 4):
            direct(j, 1, d).wait_send()
            direct(j, 2, d).wait_send()
    icore().wait_send()
    for axis in ("z", "x", "y"):
        for d in range(1, 4):
            ipeer(axis, d).wait_send()


def shards(latents, cotangent, frames, heights, widths, bucket_ids, w_in, w_mid):
    v = pltpu.VMEM
    dma = pltpu.SemaphoreType.DMA
    vm = pl.BlockSpec(memory_space=pltpu.VMEM)
    sm = pl.BlockSpec(memory_space=pltpu.SMEM)
    dec, gin, gmid = pl.pallas_call(
        kernel,
        out_shape=(
            jax.ShapeDtypeStruct((32, 12288), BF),
            jax.ShapeDtypeStruct((16, 128), F32),
            jax.ShapeDtypeStruct((264, 128), F32),
        ),
        in_specs=[sm, sm, sm, sm, vm, vm, vm, pl.BlockSpec(memory_space=pl.ANY)],
        out_specs=(vm, vm, vm),
        scratch_shapes=[
            v((10368, C), BF), v((768, 1536), BF), v((256, 256), BF), v((256, 256), BF), v((64, 256), F32),
            v((128, 256), BF), v((256, 256), F32), v((512, 256), BF), v((256, C), F32),
            v((256, C), BF), v((256, C), BF), v((256, C), BF), v((256, C), BF), v((256, 1152), F32),
            v((1152, 512), BF), v((256, 1152), F32), v((768, 1152), BF), v((768, C), BF), v((128, 1536), BF),
            v((256, 1536), F32), v((448, C), F32), v((2, 4, GROWS, C), BF), v((4, GROWS, C), BF),
            v((4, GROWS, C), F32), v((4, GROWS, C), BF), v((3, GROWS, C), BF), v((GROWS, C), F32), v((GROWS, C), BF),
            v((3, 32, C), BF), v((32, C), F32), v((32, C), BF), v((3, 32, C), BF), v((3, 4, ROWS, 128), BF),
            v((64, PIECE, 128), BF),
            v((656, 128), BF), v((640, 128), BF), v((ROWS, 128), BF), v((ROWS, 128), BF),
            v((2, 336, 128), BF), v((2, 336, 128), BF), v((4, 336, 128), BF), v((4, 336, 128), BF),
            v((8, PIECE, 128), BF), v((8, PIECE, 128), BF), v((16, PIECE, 128), BF), v((16, PIECE, 128), BF),
            v((48, PIECE, 128), F32), v((48, PIECE, 128), BF), v((9, 4, PIECE, 128), BF), v((12, PIECE, 128), F32),
            v((9, PIECE, 128), F32), v((3, PIECE + 8, 128), F32), v((104, 128), F32), v((2048, 1152), BF),
            v((1024, C), F32),
            dma((9,)), dma((16,)), dma((16,)), dma((2,)), dma((2,)), dma((18,)), dma((18,)), dma((18,)), dma((18,)),
            dma((10,)), dma((10,)),
        ],
        compiler_params=pltpu.CompilerParams(
            collective_id=0, has_side_effects=True, vmem_limit_bytes=62 * 1024 * 1024),
    )(bucket_ids, frames, heights, widths, latents, cotangent, w_in, w_mid)
    return (dec, gin.reshape(-1)[:1296], gmid.reshape(-1)[:31104])


def solution(mesh):
    return jax.shard_map(
        shards,
        mesh=mesh,
        in_specs=(
            P(("loader", "bucket"), None),
            P(("loader", "bucket"), None),
            P(("loader", "bucket")),
            P(("loader", "bucket")),
            P(("loader", "bucket")),
            P(("loader", "bucket")),
            P(),
            P(),
        ),
        out_specs=(P(("loader", "bucket"), None), P(("loader", "bucket")), P(("loader", "bucket"))),
        check_vma=False,
    )
```

```python
import math

import jax
import jax.numpy as jnp
from jax import lax
from jax.experimental import pallas as pl
from jax.experimental.pallas import tpu as pltpu
from jax.sharding import PartitionSpec as P

Z = 16
C = 384
TAPS = 27
TF = 2
TH = 4
TW = 4
CAP = 2
EPS = 1e-06
BF = jnp.bfloat16
F32 = jnp.float32
MESH = pl.DeviceIdType.MESH
ORDERS = (("z", "x", "y"), ("x", "y", "z"), ("y", "z", "x"))
ROWS = 1296
FACTOR = 1.0 / math.sqrt(1024 * TF * TH * TW)
PIECE = 96
GROWS = 80


def al(v, m):
    return pl.multiple_of(v, m)


def kernel(
    ids_ref, fra_ref, hei_ref, wid_ref, lat_hbm, cot_hbm, win_hbm, wmid_ref,
    dec_hbm, gin_ref, gmid_ref,
    w, we, snd, rcv, xsf, xsp, xbf, xbp, hf, ub, gb, ru, rg, uef, ut, gyef, gyep, gyes, ghs, df, gif, gib, rgi, gz, gzb,
    rz, gx, gxb, rx, gyv, gyb, ry, g, s1, pa0, pb0, fl0, fr0, pa1, pb1, fl1, fr1, pa2, pb2, fl2, fr2, s2f, s2, f2,
    s3, f3, fm, fo, fg, ud, acc, lat_ref, cot_ref, win_ref, dec_ref,
    o_sem, w_sem, a_send, a_recv, c_send, c_recv, r_send, r_recv, d_send, d_recv, i_send, i_recv,
):
    load = lax.axis_index("loader")
    q = lax.axis_index("bucket")
    z, c = load // 2, load % 2
    x, y = q // 4, q % 4
    pos = {"z": z, "x": x, "y": y}
    sib = (z * 2 + (1 - c), q)

    def dev(axis, v):
        if axis == "z":
            return (v * 2 + c, q)
        if axis == "x":
            return (load, v * 4 + y)
        return (load, x * 4 + v)

    def wcopy(i):
        part = pl.ds(i * 1152, 1152)
        return pltpu.make_async_copy(wmid_ref.at[part], w.at[part], w_sem.at[i])

    loads = [
        pltpu.make_async_copy(src, dst, o_sem.at[n])
        for n, (src, dst) in enumerate(((lat_hbm, lat_ref), (win_hbm, win_ref), (cot_hbm, cot_ref)))
    ]
    for load_in in loads:
        load_in.start()
    for i in range(9):
        wcopy(i).start()

    def store(f):
        lanes = slice(f * 6144, f * 6144 + 6144)
        return pltpu.make_async_copy(dec_ref.at[:, lanes], dec_hbm.at[:, lanes], o_sem.at[3 + f])

    barrier = pltpu.get_barrier_semaphore()

    @pl.loop(1, 16)
    def _(d):
        pl.semaphore_signal(barrier, 1, device_id=(load, lax.rem(q + d, 16)), device_id_type=MESH)

    for d in range(1, 4):
        pl.semaphore_signal(barrier, 1, device_id=dev("z", lax.rem(z + d, 4)), device_id_type=MESH)
    pl.semaphore_signal(barrier, 1, device_id=sib, device_id_type=MESH)

    def iota(shape, dim):
        return lax.broadcasted_iota(jnp.int32, shape, dim)

    def column(ref):
        at, out = iota((8, 1), 0), jnp.zeros((8, 1), jnp.int32)
        for t in range(8):
            out = jnp.where(at == t, ref[t], out)
        return out

    loads[0].wait()
    fra, hei, wid = column(fra_ref), column(hei_ref), column(wid_ref)
    lane = iota((8, 512), 1)
    inside = (lane // 256 < fra) & ((lane // 64) % 4 < hei) & ((lane // 16) % 4 < wid)
    xm = jnp.where(inside, lat_ref[...].astype(F32), 0.0)
    edge = jnp.zeros((8, 128), F32)
    xm = jnp.concatenate([edge, xm, edge], axis=1)
    xh = pltpu.roll(xm, 704, 1)
    lane = iota((8, 256), 1)
    for fr in range(8):
        f, r = fr // 4, fr % 4
        win = xm[:, 64 * fr + 64 : 64 * fr + 320] if fr % 2 else xh[:, 64 * fr : 64 * fr + 256]
        keep = lane < 192
        if r == 0:
            keep = keep & (lane >= 64)
        if r == 3:
            keep = keep & (lane < 128)
        ones = (lane >= 192) & (lane - 192 < wid) & (f < fra) & (r < hei)
        xsf[fr * 8 : fr * 8 + 8, :] = jnp.where(keep, win, jnp.where(ones, 1.0, 0.0))
    xs = xsf[...].astype(BF)

    def acopy(d):
        to = lax.rem(q + d, 16)
        return pltpu.make_async_remote_copy(
            snd.at[pl.ds(al(to * 16, 16), 16)], rcv.at[pl.ds(al(q * 16, 16), 16)],
            a_send.at[d], a_recv.at[d], device_id=(load, to), device_id_type=MESH)

    def afrom(d):
        src = lax.rem(q - d + 16, 16)
        rows = pl.ds(al(src * 16, 16), 16)
        return pltpu.make_async_remote_copy(
            snd.at[rows], rcv.at[rows], a_send.at[d], a_recv.at[d], device_id=(load, src), device_id_type=MESH)

    we[...] = jnp.zeros_like(we)
    loads[1].wait()
    for a in range(3):
        for b in range(3):
            for cc in range(4):
                for e in range(3):
                    ci = cc + e - 1
                    if 0 <= ci < 4:
                        we[a * 256 + (b * 4 + ci) * 16 : a * 256 + (b * 4 + ci) * 16 + 16, cc * C : cc * C + C] = (
                            win_ref[(a * 9 + b * 3 + e) * 16 : (a * 9 + b * 3 + e) * 16 + 16, :])

    xsp[0:64, :] = jnp.zeros((64, 256), BF)
    xsp[64:128, :] = xs
    h = jnp.dot(xsp[0:64, :], we[0:256, :], preferred_element_type=F32)
    h += jnp.dot(xsp[32:96, :], we[256:512, :], preferred_element_type=F32)
    h += jnp.dot(xsp[64:128, :], we[512:768, :], preferred_element_type=F32)
    for fr in range(8):
        for cc in range(4):
            hf[(fr * 4 + cc) * 8 : (fr * 4 + cc) * 8 + 8, :] = h[fr * 8 : fr * 8 + 8, cc * C : cc * C + C]

    def act(hv):
        rr = lax.rsqrt(jnp.mean(hv * hv, axis=-1, keepdims=True) + EPS)
        gv = hv * rr
        sg = jax.nn.sigmoid(gv)
        return rr, gv, sg

    rr, gn, sg = act(hf[...])
    u = gn * sg
    ub[...] = u.astype(BF)
    loads[2].wait()
    cot = cot_ref[...].astype(F32)
    for p in range(32):
        inside = (p // 16 < fra) & ((p // 4) % 4 < hei) & (p % 4 < wid)
        gyef[p * 8 : p * 8 + 8, C : 2 * C] = jnp.where(inside, cot[:, p * C : p * C + C], 0.0)
    gb[...] = gyef[:, C : 2 * C].astype(BF)

    def swap(n):
        src, dst = ((ub, ru), (gb, rg))[n]
        return pltpu.make_async_remote_copy(
            src, dst, c_send.at[n], c_recv.at[n], device_id=sib, device_id_type=MESH)

    pl.semaphore_wait(barrier, 19)
    swap(0).start()
    swap(1).start()

    ids = [ids_ref[t] for t in range(8)]
    lane, row = iota((1, 64), 1), iota((256, 64), 0)
    slots = jnp.zeros((1, 64), jnp.int32)
    for t in range(8):
        rank = jnp.int32(0)
        for before in range(t):
            rank += jnp.where(ids[before] == ids[t], 1, 0)
        slots = jnp.where(lane % 8 == t, ids[t] * CAP + rank, slots)
    pick = (row // 16 * 2 + row % 2 == slots) & ((row // 2) % 8 == lane // 8)
    snd[...] = jnp.dot(jnp.where(pick, 1.0, 0.0).astype(BF), xs, preferred_element_type=F32).astype(BF)

    @pl.loop(1, 16)
    def _(d):
        acopy(d).start()

    own = pl.ds(al(q * 16, 16), 16)
    rcv[own, :] = snd[own, :]

    def spread_u(uv, lanes):
        uef[:, C : 2 * C] = uv
        for fr in range(8):
            lo, hi = slice(fr * 32, fr * 32 + 24), slice(fr * 32 + 8, fr * 32 + 32)
            uef[hi, 0:C] = uef[lo, C : 2 * C]
            uef[lo, 2 * C : 3 * C] = uef[hi, C : 2 * C]
        ut[:, lanes] = uef[...].T.astype(BF)

    uef[...] = jnp.zeros_like(uef)
    spread_u(u, slice(0, 256))
    for fr in range(8):
        lo, hi = slice(fr * 32, fr * 32 + 24), slice(fr * 32 + 8, fr * 32 + 32)
        gyef[lo, 0:C] = gyef[hi, C : 2 * C]
        gyef[fr * 32 + 24 : fr * 32 + 32, 0:C] = jnp.zeros((8, C), F32)
        gyef[hi, 2 * C : 3 * C] = gyef[lo, C : 2 * C]
        gyef[fr * 32 : fr * 32 + 8, 2 * C : 3 * C] = jnp.zeros((8, C), F32)
    gyep[...] = jnp.zeros_like(gyep)
    gyes[...] = jnp.zeros_like(gyes)
    for f in range(2):
        gyep[(f * 6 + 1) * 32 : (f * 6 + 5) * 32, :] = gyef[f * 128 : f * 128 + 128, :].astype(BF)
    swap(0).wait_recv()
    spread_u(ru[...].astype(F32), slice(256, 512))
    swap(1).wait_recv()
    for f in range(2):
        gyes[(f * 6 + 1) * 32 : (f * 6 + 5) * 32, :] = rg[f * 128 : f * 128 + 128, :]

    def shifted(ref, i, lanes):
        a, b = i // 3, i % 3
        o0, o1 = ((2 - a) * 6 + 2 - b) * 32, ((3 - a) * 6 + 2 - b) * 32
        return jnp.concatenate([ref[o0 : o0 + 128, lanes], ref[o1 : o1 + 128, lanes]], axis=0)

    def weight_grad(zz, core):
        first = (zz * 2 + core) * ROWS
        at = first
        while at < first + ROWS:
            i = at // 1152
            lo, hi = at - i * 1152, min(1152, first + ROWS - i * 1152)
            rhs = jnp.concatenate(
                [shifted(gyep, i, slice(C, 2 * C)), shifted(gyes, i, slice(0, C))], axis=0)
            out = jnp.dot(ut[lo:hi, :], rhs, preferred_element_type=F32).astype(BF)
            for j in range(3):
                g[j, zz, at - first : at - first + hi - lo, :] = out[:, j * 128 : j * 128 + 128]
            at += hi - lo

    CUT = 656
    PIECES = (1, 2, 2)

    def own1(j, t, h, r):
        if j == 0:
            return g.at[0, t, CUT * h : (CUT, ROWS)[h]]
        if j == 1:
            return g.at[1, 2 * r + h, pl.ds(al(320 * t, 16), 336)]
        return s1.at[pl.ds(t * 16 + (2 * r + h) * 4, 4)]

    def into(j, side, h, r):
        ref = ((fl0, fr0), (fl1, fr1), (fl2, fr2))[j][side]
        if j == 0:
            return ref.at[CUT * h : (CUT, ROWS)[h]]
        if j == 1:
            return ref.at[2 * r + h]
        return ref.at[(2 * r + h) * 4 : (2 * r + h) * 4 + 4]

    def part(j, h, r):
        ref = ((pa0, pb0), (pa1, pb1), (pa2, pb2))[j][h]
        if j == 0:
            return ref
        return ref.at[r] if j == 1 else ref.at[r * 4 : r * 4 + 4]

    def target(j, n):
        return lax.rem(pos[ORDERS[j][0]] + (2, 2, 1, 3, 1, 3)[n], 4)

    def ring(j, n, r):
        axis = ORDERS[j][0]
        src, side, dst = (
            (own1(j, target(j, 0), 0, r), 1, part(j, 0, r)),
            (own1(j, target(j, 1), 1, r), 3, part(j, 1, r)),
            (own1(j, target(j, 2), 1, r), 1, into(j, 0, 1, r)),
            (own1(j, target(j, 3), 0, r), 3, into(j, 1, 0, r)),
            (part(j, 0, r), 1, into(j, 0, 0, r)),
            (part(j, 1, r), 3, into(j, 1, 1, r)),
        )[n]
        k = (j * 6 + n) * 2 + r
        return pltpu.make_async_remote_copy(
            src, dst, r_send.at[k], r_recv.at[k], device_id=dev(axis, lax.rem(pos[axis] + side, 4)),
            device_id_type=MESH)

    def relay():
        for j, r in ((1, 0), (2, 0), (0, 0), (1, 1), (2, 1)):
            for n in range(2):
                ring(j, n, r).wait_recv()
                ref = part(j, n, r)
                ref[...] = ref[...] + own1(j, target(j, 4 + n), n, r)[...]
                ring(j, 4 + n, r).start()

    for group in range(2):
        for core in range(2):

            @pl.when(c == core)
            def _():
                weight_grad(group * 2, core)
                weight_grad(group * 2 + 1, core)

        @pl.loop(0, 32)
        def _(k):
            zz, shard = group * 2 + k // 16, lax.rem(k, 16)
            s1[lax.rem(shard, 4) * 16 + zz * 4 + shard // 4] = g[2, zz, pl.ds(al(shard * 80, 16), PIECE), :]

        for n in range(4):
            for j in (2, 1):
                ring(j, n, group).start()
        for n in range(4):

            @pl.when(target(0, n) // 2 == group)
            def _():
                ring(0, n, 0).start()

    def direct(j, st, d):
        axis = ORDERS[j][st]
        to = lax.rem(pos[axis] + d, 4)
        if st == 1:
            src, dst = s2.at[pl.ds(j * 16 + to * 4, 4)], f2.at[j * 3 + d - 1]
        else:
            src, dst = s3.at[j * 4 + to], f3.at[j * 3 + d - 1]
        k = (st - 1) * 9 + j * 3 + d - 1
        return pltpu.make_async_remote_copy(
            src, dst, d_send.at[k], d_recv.at[k], device_id=dev(axis, to), device_id_type=MESH)

    def second():
        for j in range(3):
            for n in range(2, 6):
                for r in range(PIECES[j]):
                    ring(j, n, r).wait_recv()

            @pl.loop(0, 16)
            def _(k):
                if j == 0:
                    rows = pl.ds(al(k * 80, 16), PIECE)
                    terms = g[0, z, rows, :], fl0[rows, :], fr0[rows, :]
                elif j == 1:
                    yy, zz = k // 4, lax.rem(k, 4)
                    rows = pl.ds(al(yy * 80, 16), PIECE)
                    terms = g[1, zz, pl.ds(al(x * 320 + yy * 80, 16), PIECE), :], fl1[zz, rows, :], fr1[zz, rows, :]
                else:
                    terms = s1[y * 16 + k], fl2[k], fr2[k]
                total = terms[0].astype(F32) + terms[1].astype(F32) + terms[2].astype(F32)
                s2f[j * 16 + k] = total
                s2[j * 16 + k] = total.astype(BF)

            for d in (2, 1, 3):
                direct(j, 1, d).start()

    def third():
        for j in range(3):
            for d in range(1, 4):
                direct(j, 1, d).wait_recv()
            for k in range(4):
                total = s2f[j * 16 + pos[ORDERS[j][1]] * 4 + k]
                for d in range(3):
                    total += f2[j * 3 + d, k].astype(F32)
                s3[j * 4 + k] = total
            for d in (2, 1, 3):
                direct(j, 2, d).start()

    def finish():
        for j in range(3):
            for d in range(1, 4):
                direct(j, 2, d).wait_recv()
            fm[j, 0:PIECE, :] = s3[j * 4 + pos[ORDERS[j][2]]] + f3[j * 3] + f3[j * 3 + 1] + f3[j * 3 + 2]
            fm[j, PIECE:, :] = jnp.zeros((8, 128), F32)
            fo[pl.ds(j, 88, stride=3), :] = fm[j, pl.ds(q, 88), :]
        gmid_ref[...] = fo[0:243, :]


    for i in range(9):
        wcopy(i).wait()
    gu = jnp.zeros((256, C), F32)
    for i in range(9):
        for e in range(3):
            gu += lax.dot_general(
                shifted(gyep, i, slice(e * C, e * C + C)), w[i * 1152 + e * C : i * 1152 + e * C + C, :],
                (((1,), (1,)), ((), ())), preferred_element_type=F32)

    rr, gn, sg = act(hf[...])
    gv = gu * sg * (1.0 + gn * (1.0 - sg))
    gh = gyef[:, C : 2 * C] + rr * (gv - gn * jnp.mean(gv * gn, axis=-1, keepdims=True))
    hf[...] = gh
    ghs[...] = jnp.zeros_like(ghs)
    for cc in range(4):
        ghs[0:64, cc * C : cc * C + C] = jnp.concatenate(
            [hf[(fr * 4 + cc) * 8 : (fr * 4 + cc) * 8 + 8, :] for fr in range(8)], axis=0).astype(BF)
    xst = xsf[...].T.astype(BF)
    gif[...] = jnp.zeros_like(gif)
    for a in range(3):
        df[...] = jnp.dot(xst, ghs[(2 - a) * 32 : (2 - a) * 32 + 64, :], preferred_element_type=F32)
        for b in range(3):
            for e in range(3):
                total = jnp.zeros((16, C), F32)
                for cc in range(4):
                    ci = cc + e - 1
                    if 0 <= ci < 4:
                        total += df[(b * 4 + ci) * 16 : (b * 4 + ci) * 16 + 16, cc * C : cc * C + C]
                gif[(a * 9 + b * 3 + e) * 16 : (a * 9 + b * 3 + e) * 16 + 16, :] = total
    for blk in range(8):
        at = 16 * ((27 * blk) // 8)
        gib[blk % 2, blk // 2] = gif[at : at + GROWS, :].astype(BF)

    def icore():
        return pltpu.make_async_remote_copy(
            gib.at[1 - c], rgi, i_send.at[0], i_recv.at[0], device_id=sib, device_id_type=MESH)

    base = load * 54 - 16 * ((27 * load) // 8)

    def xstart(v):
        return al(16 * ((2 * base + 27 * v) // 32), 16)

    def ipeer(axis, d):
        v = lax.rem(pos[axis] + d, 4)
        src, dst, k = {
            "z": (gzb.at[v], rz.at[d - 1], 0),
            "x": (gxb.at[pl.ds(xstart(v), 32)], rx.at[d - 1], 3),
            "y": (gyb, ry.at[d - 1], 6),
        }[axis]
        return pltpu.make_async_remote_copy(
            src, dst, i_send.at[k + d], i_recv.at[k + d], device_id=dev(axis, v), device_id_type=MESH)

    def in_z():
        icore().wait_recv()
        for zz in range(4):
            at = al(16 * ((27 * (zz * 2 + c)) // 8), 16)
            total = gif[pl.ds(at, GROWS), :] + rgi[zz].astype(F32)
            gz[zz] = total
            gzb[zz] = total.astype(BF)
        for d in range(1, 4):
            ipeer("z", d).start()

    def in_x():
        for d in range(1, 4):
            ipeer("z", d).wait_recv()
        total = gz[z] + rz[0].astype(F32) + rz[1].astype(F32) + rz[2].astype(F32)
        gx[...] = total
        gxb[...] = total.astype(BF)
        for d in range(1, 4):
            ipeer("x", d).start()

    def in_y():
        for d in range(1, 4):
            ipeer("x", d).wait_recv()
        total = gx[pl.ds(xstart(x), 32), :] + rx[0].astype(F32) + rx[1].astype(F32) + rx[2].astype(F32)
        gyv[...] = total
        gyb[...] = total.astype(BF)
        for d in range(1, 4):
            ipeer("y", d).start()

    def in_end():
        for d in range(1, 4):
            ipeer("y", d).wait_recv()
        total = gyv[...] + ry[0].astype(F32) + ry[1].astype(F32) + ry[2].astype(F32)
        fg[96:, :] = jnp.zeros((8, 128), F32)
        for j in range(3):
            fg[pl.ds(j, 32, stride=3), :] = total[:, j * 128 : j * 128 + 128]
        first = 384 * (base - 16 * ((2 * base + 27 * x) // 32)) + 1296 * q
        at, lo = first // 128, lax.rem(first, 128)
        shift = lax.rem(128 - lo, 128)
        head = pltpu.roll(fg[pl.ds(at, 16), :], shift, 1)
        tail = pltpu.roll(fg[pl.ds(at + 1, 16), :], shift, 1)
        gin_ref[...] = jnp.where(iota((16, 128), 1) < 128 - lo, head, tail)

    icore().start()
    relay()
    in_z()

    @pl.loop(1, 16)
    def _(d):
        afrom(d).wait_recv()

    dst, src = iota((256, 256), 0), iota((256, 256), 1)
    order = (dst // 32 == (src // 2) % 8) & ((dst // 2) % 16 == src // 16) & (dst % 2 == src % 2)
    xbf[...] = jnp.dot(jnp.where(order, 1.0, 0.0).astype(BF), rcv[...], preferred_element_type=F32)
    xbp[0:256, :] = jnp.zeros((256, 256), BF)
    xbp[256:512, :] = xbf[...].astype(BF)
    ud[...] = jnp.zeros_like(ud)
    for f in range(2):
        hd = jnp.dot(xbp[f * 128 : f * 128 + 128, :], we[0:256, :], preferred_element_type=F32)
        hd += jnp.dot(xbp[f * 128 + 128 : f * 128 + 256, :], we[256:512, :], preferred_element_type=F32)
        hd += jnp.dot(xbp[f * 128 + 256 : f * 128 + 384, :], we[512:768, :], preferred_element_type=F32)
        for cc in range(4):
            hc = hd[:, cc * C : cc * C + C]
            _, gc, sc = act(hc)
            uc = (gc * sc).astype(BF)
            for r in range(4):
                rows = slice(r * 32, r * 32 + 32)
                acc[((f * 4 + r) * 4 + cc) * 32 : ((f * 4 + r) * 4 + cc) * 32 + 32, :] = hc[rows]
                to = (f + 2) * 512 + r * 128 + cc * 32
                for e in range(3):
                    if 0 <= cc - e + 1 < 4:
                        ud[to + (1 - e) * 32 : to + (1 - e) * 32 + 32, e * C : e * C + C] = uc[rows]

    def decode(a, f):
        taps = jnp.concatenate([w[(a * 3 + b) * 1152 : (a * 3 + b) * 1152 + 1152, :] for b in range(3)], axis=1)
        out = jnp.dot(ud[(f + a) * 512 : (f + a) * 512 + 512, :], taps, preferred_element_type=F32)
        top = f * 512
        acc[top + 128 : top + 512, :] += out[0:384, 0:C]
        acc[top : top + 512, :] += out[:, C : 2 * C]
        acc[top : top + 384, :] += out[128:512, 2 * C :]

    def emit(f):
        for p in range(16 * f, 16 * f + 16):
            m = xbf[p // 4 * 32 : p // 4 * 32 + 32, 192 + p % 4 : 193 + p % 4]
            dec_ref[:, p * C : p * C + C] = (acc[p * 32 : p * 32 + 32, :] * m).astype(BF)
        store(f).start()

    decode(0, 0)
    decode(0, 1)
    second()
    in_x()
    decode(1, 0)
    decode(1, 1)
    third()
    in_y()
    decode(2, 0)
    emit(0)
    decode(2, 1)
    emit(1)
    finish()
    in_end()

    @pl.loop(1, 16)
    def _(d):
        acopy(d).wait_send()

    store(0).wait()
    store(1).wait()
    swap(0).wait_send()
    swap(1).wait_send()
    for j in range(3):
        for n in range(6):
            for r in range(PIECES[j]):
                ring(j, n, r).wait_send()
        for d in range(1, 4):
            direct(j, 1, d).wait_send()
            direct(j, 2, d).wait_send()
    icore().wait_send()
    for axis in ("z", "x", "y"):
        for d in range(1, 4):
            ipeer(axis, d).wait_send()


def deliver(d_ref, i_ref, m_ref, dec_ref, gin_ref, gmid_ref, d_buf, i_buf, m_buf, sem):
    ins = [pltpu.make_async_copy(a, b, sem.at[n]) for n, (a, b) in enumerate(
        ((i_ref, i_buf), (m_ref, m_buf), (d_ref.at[:, 0:6144], d_buf.at[:, 0:6144]),
         (d_ref.at[:, 6144:], d_buf.at[:, 6144:])))]
    for copy in ins:
        copy.start()
    ins[0].wait()
    for n in range(10):
        gin_ref[pl.ds(n * 128, 128)] = i_buf[n, :] * FACTOR
    gin_ref[pl.ds(1280, 16)] = i_buf[10, 0:16] * FACTOR
    ins[1].wait()
    m_buf[...] = m_buf[...] * FACTOR
    outs = [pltpu.make_async_copy(a, b, sem.at[4 + n]) for n, (a, b) in enumerate(
        ((m_buf, gmid_ref), (d_buf.at[:, 0:6144], dec_ref.at[:, 0:6144]), (d_buf.at[:, 6144:], dec_ref.at[:, 6144:])))]
    outs[0].start()
    for n in (1, 2):
        ins[n + 1].wait()
        outs[n].start()
    for copy in outs:
        copy.wait()


def shards(latents, cotangent, frames, heights, widths, bucket_ids, w_in, w_mid):
    v = pltpu.VMEM
    dma = pltpu.SemaphoreType.DMA
    vm = pl.BlockSpec(memory_space=pltpu.VMEM)
    sm = pl.BlockSpec(memory_space=pltpu.SMEM)
    hbm = pl.BlockSpec(memory_space=pl.ANY)
    dec, gin, gmid = pl.pallas_call(
        kernel,
        out_shape=(
            jax.ShapeDtypeStruct((32, 12288), BF),
            jax.ShapeDtypeStruct((16, 128), F32),
            jax.ShapeDtypeStruct((243, 128), F32),
        ),
        in_specs=[sm, sm, sm, sm, hbm, hbm, hbm, hbm],
        out_specs=(hbm, vm, vm),
        scratch_shapes=[
            v((10368, C), BF), v((768, 1536), BF), v((256, 256), BF), v((256, 256), BF), v((64, 256), F32),
            v((128, 256), BF), v((256, 256), F32), v((512, 256), BF), v((256, C), F32),
            v((256, C), BF), v((256, C), BF), v((256, C), BF), v((256, C), BF), v((256, 1152), F32),
            v((1152, 512), BF), v((256, 1152), F32), v((768, 1152), BF), v((768, C), BF), v((128, 1536), BF),
            v((256, 1536), F32), v((448, C), F32), v((2, 4, GROWS, C), BF), v((4, GROWS, C), BF),
            v((4, GROWS, C), F32), v((4, GROWS, C), BF), v((3, GROWS, C), BF), v((GROWS, C), F32), v((GROWS, C), BF),
            v((3, 32, C), BF), v((32, C), F32), v((32, C), BF), v((3, 32, C), BF), v((3, 4, ROWS, 128), BF),
            v((64, PIECE, 128), BF),
            v((656, 128), BF), v((640, 128), BF), v((ROWS, 128), BF), v((ROWS, 128), BF),
            v((2, 336, 128), BF), v((2, 336, 128), BF), v((4, 336, 128), BF), v((4, 336, 128), BF),
            v((8, PIECE, 128), BF), v((8, PIECE, 128), BF), v((16, PIECE, 128), BF), v((16, PIECE, 128), BF),
            v((48, PIECE, 128), F32), v((48, PIECE, 128), BF), v((9, 4, PIECE, 128), BF), v((12, PIECE, 128), F32),
            v((9, PIECE, 128), F32), v((3, PIECE + 8, 128), F32), v((264, 128), F32), v((104, 128), F32),
            v((2048, 1152), BF), v((1024, C), F32), v((8, 512), BF), v((8, 12288), BF), v((432, C), BF), v((32, 12288), BF),
            dma((5,)), dma((9,)), dma((16,)), dma((16,)), dma((2,)), dma((2,)), dma((36,)), dma((36,)), dma((18,)), dma((18,)),
            dma((10,)), dma((10,)),
        ],
        compiler_params=pltpu.CompilerParams(
            collective_id=0, has_side_effects=True, vmem_limit_bytes=62 * 1024 * 1024),
    )(bucket_ids, frames, heights, widths, latents, cotangent, w_in, w_mid)
    dec, gin, gmid = pl.pallas_call(
        deliver,
        out_shape=(
            jax.ShapeDtypeStruct((32, 12288), BF),
            jax.ShapeDtypeStruct((1296,), F32),
            jax.ShapeDtypeStruct((243, 128), F32),
        ),
        in_specs=[hbm, hbm, hbm],
        out_specs=(hbm, vm, hbm),
        scratch_shapes=[v((32, 12288), BF), v((16, 128), F32), v((243, 128), F32), dma((7,))],
    )(dec, gin, gmid)
    return (dec, gin, gmid.reshape(-1))


def solution(mesh):
    return jax.shard_map(
        shards,
        mesh=mesh,
        in_specs=(
            P(("loader", "bucket"), None),
            P(("loader", "bucket"), None),
            P(("loader", "bucket")),
            P(("loader", "bucket")),
            P(("loader", "bucket")),
            P(("loader", "bucket")),
            P(),
            P(),
        ),
        out_specs=(P(("loader", "bucket"), None), P(("loader", "bucket")), P(("loader", "bucket"))),
        check_vma=False,
    )
```

```python
import math

import jax
import jax.numpy as jnp
from jax import lax
from jax.experimental import pallas as pl
from jax.experimental.pallas import tpu as pltpu
from jax.sharding import PartitionSpec as P

Z = 16
C = 384
TAPS = 27
TF = 2
TH = 4
TW = 4
CAP = 2
EPS = 1e-06
BF = jnp.bfloat16
F32 = jnp.float32
MESH = pl.DeviceIdType.MESH
ORDERS = (("z", "x", "y"), ("x", "y", "z"), ("y", "z", "x"))
ROWS = 1296
FACTOR = 1.0 / math.sqrt(1024 * TF * TH * TW)
PIECE = 96
GROWS = 80


def al(v, m):
    return pl.multiple_of(v, m)


def kernel(
    ids_ref, fra_ref, hei_ref, wid_ref, lat_hbm, cot_hbm, win_hbm, wmid_ref,
    dec_hbm, gin_ref, gmid_ref,
    w, we, snd, rcv, xsf, xsp, xbf, xbp, hf, ub, gb, ru, rg, uef, ut, gyef, gyep, gyes, ghs, df, gif, gib, rgi, gz, gzb,
    rz, gx, gxb, rx, gyv, gyb, ry, g, s1, pa0, pb0, fl0, fr0, pa1, pb1, fl1, fr1, pa2, pb2, fl2, fr2, s2f, s2, f2,
    s3, f3, fm, fo, fg, ud, acc, lat_ref, cot_ref, win_ref, dec_ref,
    o_sem, w_sem, a_send, a_recv, c_send, c_recv, r_send, r_recv, d_send, d_recv, i_send, i_recv,
):
    load = lax.axis_index("loader")
    q = lax.axis_index("bucket")
    z, c = load // 2, load % 2
    x, y = q // 4, q % 4
    pos = {"z": z, "x": x, "y": y}
    sib = (z * 2 + (1 - c), q)

    def dev(axis, v):
        if axis == "z":
            return (v * 2 + c, q)
        if axis == "x":
            return (load, v * 4 + y)
        return (load, x * 4 + v)

    def wcopy(i):
        part = pl.ds(i * 1152, 1152)
        return pltpu.make_async_copy(wmid_ref.at[part], w.at[part], w_sem.at[i])

    loads = [
        pltpu.make_async_copy(src, dst, o_sem.at[n])
        for n, (src, dst) in enumerate(((lat_hbm, lat_ref), (win_hbm, win_ref), (cot_hbm, cot_ref)))
    ]
    for load_in in loads:
        load_in.start()
    for i in range(9):
        wcopy(i).start()

    def store(f):
        lanes = slice(f * 6144, f * 6144 + 6144)
        return pltpu.make_async_copy(dec_ref.at[:, lanes], dec_hbm.at[:, lanes], o_sem.at[3 + f])

    barrier = pltpu.get_barrier_semaphore()

    @pl.loop(1, 16)
    def _(d):
        pl.semaphore_signal(barrier, 1, device_id=(load, lax.rem(q + d, 16)), device_id_type=MESH)

    for d in range(1, 4):
        pl.semaphore_signal(barrier, 1, device_id=dev("z", lax.rem(z + d, 4)), device_id_type=MESH)
    pl.semaphore_signal(barrier, 1, device_id=sib, device_id_type=MESH)

    def iota(shape, dim):
        return lax.broadcasted_iota(jnp.int32, shape, dim)

    def column(ref):
        at, out = iota((8, 1), 0), jnp.zeros((8, 1), jnp.int32)
        for t in range(8):
            out = jnp.where(at == t, ref[t], out)
        return out

    loads[0].wait()
    fra, hei, wid = column(fra_ref), column(hei_ref), column(wid_ref)
    lane = iota((8, 512), 1)
    inside = (lane // 256 < fra) & ((lane // 64) % 4 < hei) & ((lane // 16) % 4 < wid)
    xm = jnp.where(inside, lat_ref[...].astype(F32), 0.0)
    edge = jnp.zeros((8, 128), F32)
    xm = jnp.concatenate([edge, xm, edge], axis=1)
    xh = pltpu.roll(xm, 704, 1)
    lane = iota((8, 256), 1)
    for fr in range(8):
        f, r = fr // 4, fr % 4
        win = xm[:, 64 * fr + 64 : 64 * fr + 320] if fr % 2 else xh[:, 64 * fr : 64 * fr + 256]
        keep = lane < 192
        if r == 0:
            keep = keep & (lane >= 64)
        if r == 3:
            keep = keep & (lane < 128)
        ones = (lane >= 192) & (lane - 192 < wid) & (f < fra) & (r < hei)
        xsf[fr * 8 : fr * 8 + 8, :] = jnp.where(keep, win, jnp.where(ones, 1.0, 0.0))
    xs = xsf[...].astype(BF)

    def acopy(d):
        to = lax.rem(q + d, 16)
        return pltpu.make_async_remote_copy(
            snd.at[pl.ds(al(to * 16, 16), 16)], rcv.at[pl.ds(al(q * 16, 16), 16)],
            a_send.at[d], a_recv.at[d], device_id=(load, to), device_id_type=MESH)

    def afrom(d):
        src = lax.rem(q - d + 16, 16)
        rows = pl.ds(al(src * 16, 16), 16)
        return pltpu.make_async_remote_copy(
            snd.at[rows], rcv.at[rows], a_send.at[d], a_recv.at[d], device_id=(load, src), device_id_type=MESH)

    we[...] = jnp.zeros_like(we)
    loads[1].wait()
    for a in range(3):
        for b in range(3):
            for cc in range(4):
                for e in range(3):
                    ci = cc + e - 1
                    if 0 <= ci < 4:
                        we[a * 256 + (b * 4 + ci) * 16 : a * 256 + (b * 4 + ci) * 16 + 16, cc * C : cc * C + C] = (
                            win_ref[(a * 9 + b * 3 + e) * 16 : (a * 9 + b * 3 + e) * 16 + 16, :])

    xsp[0:64, :] = jnp.zeros((64, 256), BF)
    xsp[64:128, :] = xs
    h = jnp.dot(xsp[0:64, :], we[0:256, :], preferred_element_type=F32)
    h += jnp.dot(xsp[32:96, :], we[256:512, :], preferred_element_type=F32)
    h += jnp.dot(xsp[64:128, :], we[512:768, :], preferred_element_type=F32)
    for fr in range(8):
        for cc in range(4):
            hf[(fr * 4 + cc) * 8 : (fr * 4 + cc) * 8 + 8, :] = h[fr * 8 : fr * 8 + 8, cc * C : cc * C + C]

    def act(hv):
        rr = lax.rsqrt(jnp.mean(hv * hv, axis=-1, keepdims=True) + EPS)
        gv = hv * rr
        sg = jax.nn.sigmoid(gv)
        return rr, gv, sg

    rr, gn, sg = act(hf[...])
    u = gn * sg
    ub[...] = u.astype(BF)
    loads[2].wait()
    cot = cot_ref[...].astype(F32)
    for p in range(32):
        inside = (p // 16 < fra) & ((p // 4) % 4 < hei) & (p % 4 < wid)
        gyef[p * 8 : p * 8 + 8, C : 2 * C] = jnp.where(inside, cot[:, p * C : p * C + C], 0.0)
    gb[...] = gyef[:, C : 2 * C].astype(BF)

    def swap(n):
        src, dst = ((ub, ru), (gb, rg))[n]
        return pltpu.make_async_remote_copy(
            src, dst, c_send.at[n], c_recv.at[n], device_id=sib, device_id_type=MESH)

    pl.semaphore_wait(barrier, 19)
    swap(0).start()
    swap(1).start()

    ids = [ids_ref[t] for t in range(8)]
    lane, row = iota((1, 64), 1), iota((256, 64), 0)
    slots = jnp.zeros((1, 64), jnp.int32)
    for t in range(8):
        rank = jnp.int32(0)
        for before in range(t):
            rank += jnp.where(ids[before] == ids[t], 1, 0)
        slots = jnp.where(lane % 8 == t, ids[t] * CAP + rank, slots)
    pick = (row // 16 * 2 + row % 2 == slots) & ((row // 2) % 8 == lane // 8)
    snd[...] = jnp.dot(jnp.where(pick, 1.0, 0.0).astype(BF), xs, preferred_element_type=F32).astype(BF)

    @pl.loop(1, 16)
    def _(d):
        acopy(d).start()

    own = pl.ds(al(q * 16, 16), 16)
    rcv[own, :] = snd[own, :]

    def spread_u(uv, lanes):
        uef[:, C : 2 * C] = uv
        for fr in range(8):
            lo, hi = slice(fr * 32, fr * 32 + 24), slice(fr * 32 + 8, fr * 32 + 32)
            uef[hi, 0:C] = uef[lo, C : 2 * C]
            uef[lo, 2 * C : 3 * C] = uef[hi, C : 2 * C]
        ut[:, lanes] = uef[...].T.astype(BF)

    uef[...] = jnp.zeros_like(uef)
    spread_u(u, slice(0, 256))
    for fr in range(8):
        lo, hi = slice(fr * 32, fr * 32 + 24), slice(fr * 32 + 8, fr * 32 + 32)
        gyef[lo, 0:C] = gyef[hi, C : 2 * C]
        gyef[fr * 32 + 24 : fr * 32 + 32, 0:C] = jnp.zeros((8, C), F32)
        gyef[hi, 2 * C : 3 * C] = gyef[lo, C : 2 * C]
        gyef[fr * 32 : fr * 32 + 8, 2 * C : 3 * C] = jnp.zeros((8, C), F32)
    gyep[...] = jnp.zeros_like(gyep)
    gyes[...] = jnp.zeros_like(gyes)
    for f in range(2):
        gyep[(f * 6 + 1) * 32 : (f * 6 + 5) * 32, :] = gyef[f * 128 : f * 128 + 128, :].astype(BF)
    swap(0).wait_recv()
    spread_u(ru[...].astype(F32), slice(256, 512))
    swap(1).wait_recv()
    for f in range(2):
        gyes[(f * 6 + 1) * 32 : (f * 6 + 5) * 32, :] = rg[f * 128 : f * 128 + 128, :]

    def shifted(ref, i, lanes):
        a, b = i // 3, i % 3
        o0, o1 = ((2 - a) * 6 + 2 - b) * 32, ((3 - a) * 6 + 2 - b) * 32
        return jnp.concatenate([ref[o0 : o0 + 128, lanes], ref[o1 : o1 + 128, lanes]], axis=0)

    def weight_grad(zz, core):
        first = (zz * 2 + core) * ROWS
        at = first
        while at < first + ROWS:
            i = at // 1152
            lo, hi = at - i * 1152, min(1152, first + ROWS - i * 1152)
            rhs = jnp.concatenate(
                [shifted(gyep, i, slice(C, 2 * C)), shifted(gyes, i, slice(0, C))], axis=0)
            out = jnp.dot(ut[lo:hi, :], rhs, preferred_element_type=F32).astype(BF)
            for j in range(3):
                g[j, zz, at - first : at - first + hi - lo, :] = out[:, j * 128 : j * 128 + 128]
            at += hi - lo

    CUT = 656
    PIECES = (1, 2, 2)

    def own1(j, t, h, r):
        if j == 0:
            return g.at[0, t, CUT * h : (CUT, ROWS)[h]]
        if j == 1:
            return g.at[1, 2 * r + h, pl.ds(al(320 * t, 16), 336)]
        return s1.at[pl.ds(t * 16 + (2 * r + h) * 4, 4)]

    def into(j, side, h, r):
        ref = ((fl0, fr0), (fl1, fr1), (fl2, fr2))[j][side]
        if j == 0:
            return ref.at[CUT * h : (CUT, ROWS)[h]]
        if j == 1:
            return ref.at[2 * r + h]
        return ref.at[(2 * r + h) * 4 : (2 * r + h) * 4 + 4]

    def part(j, h, r):
        ref = ((pa0, pb0), (pa1, pb1), (pa2, pb2))[j][h]
        if j == 0:
            return ref
        return ref.at[r] if j == 1 else ref.at[r * 4 : r * 4 + 4]

    def target(j, n):
        return lax.rem(pos[ORDERS[j][0]] + (2, 2, 1, 3, 1, 3)[n], 4)

    def ring(j, n, r):
        axis = ORDERS[j][0]
        src, side, dst = (
            (own1(j, target(j, 0), 0, r), 1, part(j, 0, r)),
            (own1(j, target(j, 1), 1, r), 3, part(j, 1, r)),
            (own1(j, target(j, 2), 1, r), 1, into(j, 0, 1, r)),
            (own1(j, target(j, 3), 0, r), 3, into(j, 1, 0, r)),
            (part(j, 0, r), 1, into(j, 0, 0, r)),
            (part(j, 1, r), 3, into(j, 1, 1, r)),
        )[n]
        k = (j * 6 + n) * 2 + r
        return pltpu.make_async_remote_copy(
            src, dst, r_send.at[k], r_recv.at[k], device_id=dev(axis, lax.rem(pos[axis] + side, 4)),
            device_id_type=MESH)

    def relay():
        for j, r in ((1, 0), (2, 0), (0, 0), (1, 1), (2, 1)):
            for n in range(2):
                ring(j, n, r).wait_recv()
                ref = part(j, n, r)
                ref[...] = ref[...] + own1(j, target(j, 4 + n), n, r)[...]
                ring(j, 4 + n, r).start()

    for group in range(2):
        for core in range(2):

            @pl.when(c == core)
            def _():
                weight_grad(group * 2, core)
                weight_grad(group * 2 + 1, core)

        @pl.loop(0, 32)
        def _(k):
            zz, shard = group * 2 + k // 16, lax.rem(k, 16)
            s1[lax.rem(shard, 4) * 16 + zz * 4 + shard // 4] = g[2, zz, pl.ds(al(shard * 80, 16), PIECE), :]

        for n in range(4):
            for j in (2, 1):
                ring(j, n, group).start()
        for n in range(4):

            @pl.when(target(0, n) // 2 == group)
            def _():
                ring(0, n, 0).start()

    def direct(j, st, d):
        axis = ORDERS[j][st]
        to = lax.rem(pos[axis] + d, 4)
        if st == 1:
            src, dst = s2.at[pl.ds(j * 16 + to * 4, 4)], f2.at[j * 3 + d - 1]
        else:
            src, dst = s3.at[j * 4 + to], f3.at[j * 3 + d - 1]
        k = (st - 1) * 9 + j * 3 + d - 1
        return pltpu.make_async_remote_copy(
            src, dst, d_send.at[k], d_recv.at[k], device_id=dev(axis, to), device_id_type=MESH)

    def second():
        for j in range(3):
            for n in range(2, 6):
                for r in range(PIECES[j]):
                    ring(j, n, r).wait_recv()

            @pl.loop(0, 16)
            def _(k):
                if j == 0:
                    rows = pl.ds(al(k * 80, 16), PIECE)
                    terms = g[0, z, rows, :], fl0[rows, :], fr0[rows, :]
                elif j == 1:
                    yy, zz = k // 4, lax.rem(k, 4)
                    rows = pl.ds(al(yy * 80, 16), PIECE)
                    terms = g[1, zz, pl.ds(al(x * 320 + yy * 80, 16), PIECE), :], fl1[zz, rows, :], fr1[zz, rows, :]
                else:
                    terms = s1[y * 16 + k], fl2[k], fr2[k]
                total = terms[0].astype(F32) + terms[1].astype(F32) + terms[2].astype(F32)
                s2f[j * 16 + k] = total
                s2[j * 16 + k] = total.astype(BF)

            for d in (2, 1, 3):
                direct(j, 1, d).start()

    def third():
        for j in range(3):
            for d in range(1, 4):
                direct(j, 1, d).wait_recv()
            for k in range(4):
                total = s2f[j * 16 + pos[ORDERS[j][1]] * 4 + k]
                for d in range(3):
                    total += f2[j * 3 + d, k].astype(F32)
                s3[j * 4 + k] = total
            for d in (2, 1, 3):
                direct(j, 2, d).start()

    def finish():
        for j in range(3):
            for d in range(1, 4):
                direct(j, 2, d).wait_recv()
            fm[j, 0:PIECE, :] = s3[j * 4 + pos[ORDERS[j][2]]] + f3[j * 3] + f3[j * 3 + 1] + f3[j * 3 + 2]
            fm[j, PIECE:, :] = jnp.zeros((8, 128), F32)
            fo[pl.ds(j, 88, stride=3), :] = fm[j, pl.ds(q, 88), :]
        gmid_ref[...] = fo[0:243, :]


    for i in range(9):
        wcopy(i).wait()
    gu = jnp.zeros((256, C), F32)
    for i in range(9):
        for e in range(3):
            gu += lax.dot_general(
                shifted(gyep, i, slice(e * C, e * C + C)), w[i * 1152 + e * C : i * 1152 + e * C + C, :],
                (((1,), (1,)), ((), ())), preferred_element_type=F32)

    relay()
    rr, gn, sg = act(hf[...])
    gv = gu * sg * (1.0 + gn * (1.0 - sg))
    gh = gyef[:, C : 2 * C] + rr * (gv - gn * jnp.mean(gv * gn, axis=-1, keepdims=True))
    hf[...] = gh
    ghs[...] = jnp.zeros_like(ghs)
    for cc in range(4):
        ghs[0:64, cc * C : cc * C + C] = jnp.concatenate(
            [hf[(fr * 4 + cc) * 8 : (fr * 4 + cc) * 8 + 8, :] for fr in range(8)], axis=0).astype(BF)
    xst = xsf[...].T.astype(BF)
    gif[...] = jnp.zeros_like(gif)
    for a in range(3):
        df[...] = jnp.dot(xst, ghs[(2 - a) * 32 : (2 - a) * 32 + 64, :], preferred_element_type=F32)
        for b in range(3):
            for e in range(3):
                total = jnp.zeros((16, C), F32)
                for cc in range(4):
                    ci = cc + e - 1
                    if 0 <= ci < 4:
                        total += df[(b * 4 + ci) * 16 : (b * 4 + ci) * 16 + 16, cc * C : cc * C + C]
                gif[(a * 9 + b * 3 + e) * 16 : (a * 9 + b * 3 + e) * 16 + 16, :] = total
    for blk in range(8):
        at = 16 * ((27 * blk) // 8)
        gib[blk % 2, blk // 2] = gif[at : at + GROWS, :].astype(BF)

    def icore():
        return pltpu.make_async_remote_copy(
            gib.at[1 - c], rgi, i_send.at[0], i_recv.at[0], device_id=sib, device_id_type=MESH)

    base = load * 54 - 16 * ((27 * load) // 8)

    def xstart(v):
        return al(16 * ((2 * base + 27 * v) // 32), 16)

    def ipeer(axis, d):
        v = lax.rem(pos[axis] + d, 4)
        src, dst, k = {
            "z": (gzb.at[v], rz.at[d - 1], 0),
            "x": (gxb.at[pl.ds(xstart(v), 32)], rx.at[d - 1], 3),
            "y": (gyb, ry.at[d - 1], 6),
        }[axis]
        return pltpu.make_async_remote_copy(
            src, dst, i_send.at[k + d], i_recv.at[k + d], device_id=dev(axis, v), device_id_type=MESH)

    def in_z():
        icore().wait_recv()
        for zz in range(4):
            at = al(16 * ((27 * (zz * 2 + c)) // 8), 16)
            total = gif[pl.ds(at, GROWS), :] + rgi[zz].astype(F32)
            gz[zz] = total
            gzb[zz] = total.astype(BF)
        for d in range(1, 4):
            ipeer("z", d).start()

    def in_x():
        for d in range(1, 4):
            ipeer("z", d).wait_recv()
        total = gz[z] + rz[0].astype(F32) + rz[1].astype(F32) + rz[2].astype(F32)
        gx[...] = total
        gxb[...] = total.astype(BF)
        for d in range(1, 4):
            ipeer("x", d).start()

    def in_y():
        for d in range(1, 4):
            ipeer("x", d).wait_recv()
        total = gx[pl.ds(xstart(x), 32), :] + rx[0].astype(F32) + rx[1].astype(F32) + rx[2].astype(F32)
        gyv[...] = total
        gyb[...] = total.astype(BF)
        for d in range(1, 4):
            ipeer("y", d).start()

    def in_end():
        for d in range(1, 4):
            ipeer("y", d).wait_recv()
        total = gyv[...] + ry[0].astype(F32) + ry[1].astype(F32) + ry[2].astype(F32)
        fg[96:, :] = jnp.zeros((8, 128), F32)
        for j in range(3):
            fg[pl.ds(j, 32, stride=3), :] = total[:, j * 128 : j * 128 + 128]
        first = 384 * (base - 16 * ((2 * base + 27 * x) // 32)) + 1296 * q
        at, lo = first // 128, lax.rem(first, 128)
        shift = lax.rem(128 - lo, 128)
        head = pltpu.roll(fg[pl.ds(at, 16), :], shift, 1)
        tail = pltpu.roll(fg[pl.ds(at + 1, 16), :], shift, 1)
        gin_ref[...] = jnp.where(iota((16, 128), 1) < 128 - lo, head, tail)

    icore().start()
    in_z()

    @pl.loop(1, 16)
    def _(d):
        afrom(d).wait_recv()

    dst, src = iota((256, 256), 0), iota((256, 256), 1)
    order = (dst // 32 == (src // 2) % 8) & ((dst // 2) % 16 == src // 16) & (dst % 2 == src % 2)
    xbf[...] = jnp.dot(jnp.where(order, 1.0, 0.0).astype(BF), rcv[...], preferred_element_type=F32)
    xbp[0:256, :] = jnp.zeros((256, 256), BF)
    xbp[256:512, :] = xbf[...].astype(BF)
    ud[...] = jnp.zeros_like(ud)
    for f in range(2):
        hd = jnp.dot(xbp[f * 128 : f * 128 + 128, :], we[0:256, :], preferred_element_type=F32)
        hd += jnp.dot(xbp[f * 128 + 128 : f * 128 + 256, :], we[256:512, :], preferred_element_type=F32)
        hd += jnp.dot(xbp[f * 128 + 256 : f * 128 + 384, :], we[512:768, :], preferred_element_type=F32)
        for cc in range(4):
            hc = hd[:, cc * C : cc * C + C]
            _, gc, sc = act(hc)
            uc = (gc * sc).astype(BF)
            for r in range(4):
                rows = slice(r * 32, r * 32 + 32)
                acc[((f * 4 + r) * 4 + cc) * 32 : ((f * 4 + r) * 4 + cc) * 32 + 32, :] = hc[rows]
                to = (f + 2) * 512 + r * 128 + cc * 32
                for e in range(3):
                    if 0 <= cc - e + 1 < 4:
                        ud[to + (1 - e) * 32 : to + (1 - e) * 32 + 32, e * C : e * C + C] = uc[rows]

    def decode(a, f):
        taps = jnp.concatenate([w[(a * 3 + b) * 1152 : (a * 3 + b) * 1152 + 1152, :] for b in range(3)], axis=1)
        out = jnp.dot(ud[(f + a) * 512 : (f + a) * 512 + 512, :], taps, preferred_element_type=F32)
        top = f * 512
        acc[top + 128 : top + 512, :] += out[0:384, 0:C]
        acc[top : top + 512, :] += out[:, C : 2 * C]
        acc[top : top + 384, :] += out[128:512, 2 * C :]

    def emit(f):
        for p in range(16 * f, 16 * f + 16):
            m = xbf[p // 4 * 32 : p // 4 * 32 + 32, 192 + p % 4 : 193 + p % 4]
            dec_ref[:, p * C : p * C + C] = (acc[p * 32 : p * 32 + 32, :] * m).astype(BF)
        store(f).start()

    decode(0, 0)
    decode(0, 1)
    second()
    in_x()
    decode(1, 0)
    decode(1, 1)
    third()
    in_y()
    decode(2, 0)
    emit(0)
    decode(2, 1)
    emit(1)
    finish()
    in_end()

    @pl.loop(1, 16)
    def _(d):
        acopy(d).wait_send()

    store(0).wait()
    store(1).wait()
    swap(0).wait_send()
    swap(1).wait_send()
    for j in range(3):
        for n in range(6):
            for r in range(PIECES[j]):
                ring(j, n, r).wait_send()
        for d in range(1, 4):
            direct(j, 1, d).wait_send()
            direct(j, 2, d).wait_send()
    icore().wait_send()
    for axis in ("z", "x", "y"):
        for d in range(1, 4):
            ipeer(axis, d).wait_send()


def deliver(d_ref, i_ref, m_ref, dec_ref, gin_ref, gmid_ref, d_buf, i_buf, m_buf, sem):
    ins = [pltpu.make_async_copy(a, b, sem.at[n]) for n, (a, b) in enumerate(
        ((i_ref, i_buf), (m_ref, m_buf), (d_ref.at[:, 0:6144], d_buf.at[:, 0:6144]),
         (d_ref.at[:, 6144:], d_buf.at[:, 6144:])))]
    for copy in ins:
        copy.start()
    ins[0].wait()
    for n in range(10):
        gin_ref[pl.ds(n * 128, 128)] = i_buf[n, :] * FACTOR
    gin_ref[pl.ds(1280, 16)] = i_buf[10, 0:16] * FACTOR
    ins[1].wait()
    m_buf[...] = m_buf[...] * FACTOR
    outs = [pltpu.make_async_copy(a, b, sem.at[4 + n]) for n, (a, b) in enumerate(
        ((m_buf, gmid_ref), (d_buf.at[:, 0:6144], dec_ref.at[:, 0:6144]), (d_buf.at[:, 6144:], dec_ref.at[:, 6144:])))]
    outs[0].start()
    for n in (1, 2):
        ins[n + 1].wait()
        outs[n].start()
    for copy in outs:
        copy.wait()


def shards(latents, cotangent, frames, heights, widths, bucket_ids, w_in, w_mid):
    v = pltpu.VMEM
    dma = pltpu.SemaphoreType.DMA
    vm = pl.BlockSpec(memory_space=pltpu.VMEM)
    sm = pl.BlockSpec(memory_space=pltpu.SMEM)
    hbm = pl.BlockSpec(memory_space=pl.ANY)
    dec, gin, gmid = pl.pallas_call(
        kernel,
        out_shape=(
            jax.ShapeDtypeStruct((32, 12288), BF),
            jax.ShapeDtypeStruct((16, 128), F32),
            jax.ShapeDtypeStruct((243, 128), F32),
        ),
        in_specs=[sm, sm, sm, sm, hbm, hbm, hbm, hbm],
        out_specs=(hbm, vm, vm),
        scratch_shapes=[
            v((10368, C), BF), v((768, 1536), BF), v((256, 256), BF), v((256, 256), BF), v((64, 256), F32),
            v((128, 256), BF), v((256, 256), F32), v((512, 256), BF), v((256, C), F32),
            v((256, C), BF), v((256, C), BF), v((256, C), BF), v((256, C), BF), v((256, 1152), F32),
            v((1152, 512), BF), v((256, 1152), F32), v((768, 1152), BF), v((768, C), BF), v((128, 1536), BF),
            v((256, 1536), F32), v((448, C), F32), v((2, 4, GROWS, C), BF), v((4, GROWS, C), BF),
            v((4, GROWS, C), F32), v((4, GROWS, C), BF), v((3, GROWS, C), BF), v((GROWS, C), F32), v((GROWS, C), BF),
            v((3, 32, C), BF), v((32, C), F32), v((32, C), BF), v((3, 32, C), BF), v((3, 4, ROWS, 128), BF),
            v((64, PIECE, 128), BF),
            v((656, 128), BF), v((640, 128), BF), v((ROWS, 128), BF), v((ROWS, 128), BF),
            v((2, 336, 128), BF), v((2, 336, 128), BF), v((4, 336, 128), BF), v((4, 336, 128), BF),
            v((8, PIECE, 128), BF), v((8, PIECE, 128), BF), v((16, PIECE, 128), BF), v((16, PIECE, 128), BF),
            v((48, PIECE, 128), F32), v((48, PIECE, 128), BF), v((9, 4, PIECE, 128), BF), v((12, PIECE, 128), F32),
            v((9, PIECE, 128), F32), v((3, PIECE + 8, 128), F32), v((264, 128), F32), v((104, 128), F32),
            v((2048, 1152), BF), v((1024, C), F32), v((8, 512), BF), v((8, 12288), BF), v((432, C), BF), v((32, 12288), BF),
            dma((5,)), dma((9,)), dma((16,)), dma((16,)), dma((2,)), dma((2,)), dma((36,)), dma((36,)), dma((18,)), dma((18,)),
            dma((10,)), dma((10,)),
        ],
        compiler_params=pltpu.CompilerParams(
            collective_id=0, has_side_effects=True, vmem_limit_bytes=62 * 1024 * 1024),
    )(bucket_ids, frames, heights, widths, latents, cotangent, w_in, w_mid)
    dec, gin, gmid = pl.pallas_call(
        deliver,
        out_shape=(
            jax.ShapeDtypeStruct((32, 12288), BF),
            jax.ShapeDtypeStruct((1296,), F32),
            jax.ShapeDtypeStruct((243, 128), F32),
        ),
        in_specs=[hbm, hbm, hbm],
        out_specs=(hbm, vm, hbm),
        scratch_shapes=[v((32, 12288), BF), v((16, 128), F32), v((243, 128), F32), dma((7,))],
    )(dec, gin, gmid)
    return (dec, gin, gmid.reshape(-1))


def solution(mesh):
    return jax.shard_map(
        shards,
        mesh=mesh,
        in_specs=(
            P(("loader", "bucket"), None),
            P(("loader", "bucket"), None),
            P(("loader", "bucket")),
            P(("loader", "bucket")),
            P(("loader", "bucket")),
            P(("loader", "bucket")),
            P(),
            P(),
        ),
        out_specs=(P(("loader", "bucket"), None), P(("loader", "bucket")), P(("loader", "bucket"))),
        check_vma=False,
    )
```

```python
import math

import jax
import jax.numpy as jnp
from jax import lax
from jax.experimental import pallas as pl
from jax.experimental.pallas import tpu as pltpu
from jax.sharding import PartitionSpec as P

Z = 16
C = 384
TAPS = 27
TF = 2
TH = 4
TW = 4
CAP = 2
EPS = 1e-06
BF = jnp.bfloat16
F32 = jnp.float32
MESH = pl.DeviceIdType.MESH
ORDERS = (("z", "x", "y"), ("x", "y", "z"), ("y", "z", "x"))
ROWS = 1296
FACTOR = 1.0 / math.sqrt(1024 * TF * TH * TW)
PIECE = 96
GROWS = 80


def al(v, m):
    return pl.multiple_of(v, m)


def kernel(
    ids_ref, fra_ref, hei_ref, wid_ref, lat_hbm, cot_hbm, win_hbm, wmid_ref,
    dec_hbm, gin_ref, gmid_ref,
    w, we, snd, rcv, xsf, xsp, xbf, xbp, hf, ub, gb, ru, rg, uef, ut, gyef, gyep, gyes, ghs, df, gif, gib, rgi, gz, gzb,
    rz, gx, gxb, rx, gyv, gyb, ry, g, s1, pa0, pb0, fl0, fr0, pa1, pb1, fl1, fr1, pa2, pb2, fl2, fr2, s2f, s2, f2,
    s3, f3, fm, fo, fg, ud, acc, lat_ref, cot_ref, win_ref, dec_ref,
    o_sem, w_sem, a_send, a_recv, c_send, c_recv, r_send, r_recv, d_send, d_recv, i_send, i_recv,
):
    load = lax.axis_index("loader")
    q = lax.axis_index("bucket")
    z, c = load // 2, load % 2
    x, y = q // 4, q % 4
    pos = {"z": z, "x": x, "y": y}
    sib = (z * 2 + (1 - c), q)

    def dev(axis, v):
        if axis == "z":
            return (v * 2 + c, q)
        if axis == "x":
            return (load, v * 4 + y)
        return (load, x * 4 + v)

    def wcopy(i):
        part = pl.ds(i * 1152, 1152)
        return pltpu.make_async_copy(wmid_ref.at[part], w.at[part], w_sem.at[i])

    loads = [
        pltpu.make_async_copy(src, dst, o_sem.at[n])
        for n, (src, dst) in enumerate(((lat_hbm, lat_ref), (win_hbm, win_ref), (cot_hbm, cot_ref)))
    ]
    for load_in in loads:
        load_in.start()
    for i in range(9):
        wcopy(i).start()

    def store(f):
        lanes = slice(f * 6144, f * 6144 + 6144)
        return pltpu.make_async_copy(dec_ref.at[:, lanes], dec_hbm.at[:, lanes], o_sem.at[3 + f])

    barrier = pltpu.get_barrier_semaphore()

    @pl.loop(1, 16)
    def _(d):
        pl.semaphore_signal(barrier, 1, device_id=(load, lax.rem(q + d, 16)), device_id_type=MESH)

    for d in range(1, 4):
        pl.semaphore_signal(barrier, 1, device_id=dev("z", lax.rem(z + d, 4)), device_id_type=MESH)
    pl.semaphore_signal(barrier, 1, device_id=sib, device_id_type=MESH)

    def iota(shape, dim):
        return lax.broadcasted_iota(jnp.int32, shape, dim)

    def column(ref):
        at, out = iota((8, 1), 0), jnp.zeros((8, 1), jnp.int32)
        for t in range(8):
            out = jnp.where(at == t, ref[t], out)
        return out

    loads[0].wait()
    fra, hei, wid = column(fra_ref), column(hei_ref), column(wid_ref)
    lane = iota((8, 512), 1)
    inside = (lane // 256 < fra) & ((lane // 64) % 4 < hei) & ((lane // 16) % 4 < wid)
    xm = jnp.where(inside, lat_ref[...].astype(F32), 0.0)
    edge = jnp.zeros((8, 128), F32)
    xm = jnp.concatenate([edge, xm, edge], axis=1)
    xh = pltpu.roll(xm, 704, 1)
    lane = iota((8, 256), 1)
    for fr in range(8):
        f, r = fr // 4, fr % 4
        win = xm[:, 64 * fr + 64 : 64 * fr + 320] if fr % 2 else xh[:, 64 * fr : 64 * fr + 256]
        keep = lane < 192
        if r == 0:
            keep = keep & (lane >= 64)
        if r == 3:
            keep = keep & (lane < 128)
        ones = (lane >= 192) & (lane - 192 < wid) & (f < fra) & (r < hei)
        xsf[fr * 8 : fr * 8 + 8, :] = jnp.where(keep, win, jnp.where(ones, 1.0, 0.0))
    xs = xsf[...].astype(BF)

    def acopy(d):
        to = lax.rem(q + d, 16)
        return pltpu.make_async_remote_copy(
            snd.at[pl.ds(al(to * 16, 16), 16)], rcv.at[pl.ds(al(q * 16, 16), 16)],
            a_send.at[d], a_recv.at[d], device_id=(load, to), device_id_type=MESH)

    def afrom(d):
        src = lax.rem(q - d + 16, 16)
        rows = pl.ds(al(src * 16, 16), 16)
        return pltpu.make_async_remote_copy(
            snd.at[rows], rcv.at[rows], a_send.at[d], a_recv.at[d], device_id=(load, src), device_id_type=MESH)

    we[...] = jnp.zeros_like(we)
    loads[1].wait()
    for a in range(3):
        for b in range(3):
            for cc in range(4):
                for e in range(3):
                    ci = cc + e - 1
                    if 0 <= ci < 4:
                        we[a * 256 + (b * 4 + ci) * 16 : a * 256 + (b * 4 + ci) * 16 + 16, cc * C : cc * C + C] = (
                            win_ref[(a * 9 + b * 3 + e) * 16 : (a * 9 + b * 3 + e) * 16 + 16, :])

    xsp[0:64, :] = jnp.zeros((64, 256), BF)
    xsp[64:128, :] = xs
    h = jnp.dot(xsp[0:64, :], we[0:256, :], preferred_element_type=F32)
    h += jnp.dot(xsp[32:96, :], we[256:512, :], preferred_element_type=F32)
    h += jnp.dot(xsp[64:128, :], we[512:768, :], preferred_element_type=F32)
    for fr in range(8):
        for cc in range(4):
            hf[(fr * 4 + cc) * 8 : (fr * 4 + cc) * 8 + 8, :] = h[fr * 8 : fr * 8 + 8, cc * C : cc * C + C]

    def act(hv):
        rr = lax.rsqrt(jnp.mean(hv * hv, axis=-1, keepdims=True) + EPS)
        gv = hv * rr
        sg = jax.nn.sigmoid(gv)
        return rr, gv, sg

    rr, gn, sg = act(hf[...])
    u = gn * sg
    ub[...] = u.astype(BF)
    loads[2].wait()
    cot = cot_ref[...].astype(F32)
    for p in range(32):
        inside = (p // 16 < fra) & ((p // 4) % 4 < hei) & (p % 4 < wid)
        gyef[p * 8 : p * 8 + 8, C : 2 * C] = jnp.where(inside, cot[:, p * C : p * C + C], 0.0)
    gb[...] = gyef[:, C : 2 * C].astype(BF)

    def swap(n):
        src, dst = ((ub, ru), (gb, rg))[n]
        return pltpu.make_async_remote_copy(
            src, dst, c_send.at[n], c_recv.at[n], device_id=sib, device_id_type=MESH)

    pl.semaphore_wait(barrier, 19)
    swap(0).start()
    swap(1).start()

    ids = [ids_ref[t] for t in range(8)]
    lane, row = iota((1, 64), 1), iota((256, 64), 0)
    slots = jnp.zeros((1, 64), jnp.int32)
    for t in range(8):
        rank = jnp.int32(0)
        for before in range(t):
            rank += jnp.where(ids[before] == ids[t], 1, 0)
        slots = jnp.where(lane % 8 == t, ids[t] * CAP + rank, slots)
    pick = (row // 16 * 2 + row % 2 == slots) & ((row // 2) % 8 == lane // 8)
    snd[...] = jnp.dot(jnp.where(pick, 1.0, 0.0).astype(BF), xs, preferred_element_type=F32).astype(BF)

    @pl.loop(1, 16)
    def _(d):
        acopy(d).start()

    own = pl.ds(al(q * 16, 16), 16)
    rcv[own, :] = snd[own, :]

    def spread_u(uv, lanes):
        uef[:, C : 2 * C] = uv
        for fr in range(8):
            lo, hi = slice(fr * 32, fr * 32 + 24), slice(fr * 32 + 8, fr * 32 + 32)
            uef[hi, 0:C] = uef[lo, C : 2 * C]
            uef[lo, 2 * C : 3 * C] = uef[hi, C : 2 * C]
        ut[:, lanes] = uef[...].T.astype(BF)

    uef[...] = jnp.zeros_like(uef)
    spread_u(u, slice(0, 256))
    for fr in range(8):
        lo, hi = slice(fr * 32, fr * 32 + 24), slice(fr * 32 + 8, fr * 32 + 32)
        gyef[lo, 0:C] = gyef[hi, C : 2 * C]
        gyef[fr * 32 + 24 : fr * 32 + 32, 0:C] = jnp.zeros((8, C), F32)
        gyef[hi, 2 * C : 3 * C] = gyef[lo, C : 2 * C]
        gyef[fr * 32 : fr * 32 + 8, 2 * C : 3 * C] = jnp.zeros((8, C), F32)
    gyep[...] = jnp.zeros_like(gyep)
    gyes[...] = jnp.zeros_like(gyes)
    for f in range(2):
        gyep[(f * 6 + 1) * 32 : (f * 6 + 5) * 32, :] = gyef[f * 128 : f * 128 + 128, :].astype(BF)
    swap(0).wait_recv()
    spread_u(ru[...].astype(F32), slice(256, 512))
    swap(1).wait_recv()
    for f in range(2):
        gyes[(f * 6 + 1) * 32 : (f * 6 + 5) * 32, :] = rg[f * 128 : f * 128 + 128, :]

    def shifted(ref, i, lanes):
        a, b = i // 3, i % 3
        o0, o1 = ((2 - a) * 6 + 2 - b) * 32, ((3 - a) * 6 + 2 - b) * 32
        return jnp.concatenate([ref[o0 : o0 + 128, lanes], ref[o1 : o1 + 128, lanes]], axis=0)

    def weight_grad(zz, core):
        first = (zz * 2 + core) * ROWS
        at = first
        while at < first + ROWS:
            i = at // 1152
            lo, hi = at - i * 1152, min(1152, first + ROWS - i * 1152)
            rhs = jnp.concatenate(
                [shifted(gyep, i, slice(C, 2 * C)), shifted(gyes, i, slice(0, C))], axis=0)
            out = jnp.dot(ut[lo:hi, :], rhs, preferred_element_type=F32).astype(BF)
            for j in range(3):
                g[j, zz, at - first : at - first + hi - lo, :] = out[:, j * 128 : j * 128 + 128]
            at += hi - lo

    CUT = 656
    PIECES = (1, 2, 2)

    def own1(j, t, h, r):
        if j == 0:
            return g.at[0, t, CUT * h : (CUT, ROWS)[h]]
        if j == 1:
            return g.at[1, 2 * r + h, pl.ds(al(320 * t, 16), 336)]
        return s1.at[pl.ds(t * 16 + (2 * r + h) * 4, 4)]

    def into(j, side, h, r):
        ref = ((fl0, fr0), (fl1, fr1), (fl2, fr2))[j][side]
        if j == 0:
            return ref.at[CUT * h : (CUT, ROWS)[h]]
        if j == 1:
            return ref.at[2 * r + h]
        return ref.at[(2 * r + h) * 4 : (2 * r + h) * 4 + 4]

    def part(j, h, r):
        ref = ((pa0, pb0), (pa1, pb1), (pa2, pb2))[j][h]
        if j == 0:
            return ref
        return ref.at[r] if j == 1 else ref.at[r * 4 : r * 4 + 4]

    def target(j, n):
        return lax.rem(pos[ORDERS[j][0]] + (2, 2, 1, 3, 1, 3)[n], 4)

    def ring(j, n, r):
        axis = ORDERS[j][0]
        src, side, dst = (
            (own1(j, target(j, 0), 0, r), 1, part(j, 0, r)),
            (own1(j, target(j, 1), 1, r), 3, part(j, 1, r)),
            (own1(j, target(j, 2), 1, r), 1, into(j, 0, 1, r)),
            (own1(j, target(j, 3), 0, r), 3, into(j, 1, 0, r)),
            (part(j, 0, r), 1, into(j, 0, 0, r)),
            (part(j, 1, r), 3, into(j, 1, 1, r)),
        )[n]
        k = (j * 6 + n) * 2 + r
        return pltpu.make_async_remote_copy(
            src, dst, r_send.at[k], r_recv.at[k], device_id=dev(axis, lax.rem(pos[axis] + side, 4)),
            device_id_type=MESH)

    def relay(pieces):
        for j, r in pieces:
            for n in range(2):
                ring(j, n, r).wait_recv()
                ref = part(j, n, r)
                ref[...] = ref[...] + own1(j, target(j, 4 + n), n, r)[...]
                ring(j, 4 + n, r).start()

    for group in range(2):
        for core in range(2):

            @pl.when(c == core)
            def _():
                weight_grad(group * 2, core)
                weight_grad(group * 2 + 1, core)

        @pl.loop(0, 32)
        def _(k):
            zz, shard = group * 2 + k // 16, lax.rem(k, 16)
            s1[lax.rem(shard, 4) * 16 + zz * 4 + shard // 4] = g[2, zz, pl.ds(al(shard * 80, 16), PIECE), :]

        for n in range(4):
            for j in (2, 1):
                ring(j, n, group).start()
        for n in range(4):

            @pl.when(target(0, n) // 2 == group)
            def _():
                ring(0, n, 0).start()

    def direct(j, st, d):
        axis = ORDERS[j][st]
        to = lax.rem(pos[axis] + d, 4)
        if st == 1:
            src, dst = s2.at[pl.ds(j * 16 + to * 4, 4)], f2.at[j * 3 + d - 1]
        else:
            src, dst = s3.at[j * 4 + to], f3.at[j * 3 + d - 1]
        k = (st - 1) * 9 + j * 3 + d - 1
        return pltpu.make_async_remote_copy(
            src, dst, d_send.at[k], d_recv.at[k], device_id=dev(axis, to), device_id_type=MESH)

    def second():
        for j in range(3):
            for n in range(2, 6):
                for r in range(PIECES[j]):
                    ring(j, n, r).wait_recv()

            @pl.loop(0, 16)
            def _(k):
                if j == 0:
                    rows = pl.ds(al(k * 80, 16), PIECE)
                    terms = g[0, z, rows, :], fl0[rows, :], fr0[rows, :]
                elif j == 1:
                    yy, zz = k // 4, lax.rem(k, 4)
                    rows = pl.ds(al(yy * 80, 16), PIECE)
                    terms = g[1, zz, pl.ds(al(x * 320 + yy * 80, 16), PIECE), :], fl1[zz, rows, :], fr1[zz, rows, :]
                else:
                    terms = s1[y * 16 + k], fl2[k], fr2[k]
                total = terms[0].astype(F32) + terms[1].astype(F32) + terms[2].astype(F32)
                s2f[j * 16 + k] = total
                s2[j * 16 + k] = total.astype(BF)

            for d in (2, 1, 3):
                direct(j, 1, d).start()

    def third():
        for j in range(3):
            for d in range(1, 4):
                direct(j, 1, d).wait_recv()
            for k in range(4):
                total = s2f[j * 16 + pos[ORDERS[j][1]] * 4 + k]
                for d in range(3):
                    total += f2[j * 3 + d, k].astype(F32)
                s3[j * 4 + k] = total
            for d in (2, 1, 3):
                direct(j, 2, d).start()

    def finish():
        for j in range(3):
            for d in range(1, 4):
                direct(j, 2, d).wait_recv()
            fm[j, 0:PIECE, :] = s3[j * 4 + pos[ORDERS[j][2]]] + f3[j * 3] + f3[j * 3 + 1] + f3[j * 3 + 2]
            fm[j, PIECE:, :] = jnp.zeros((8, 128), F32)
            fo[pl.ds(j, 88, stride=3), :] = fm[j, pl.ds(q, 88), :]
        gmid_ref[...] = fo[0:243, :]


    for i in range(9):
        wcopy(i).wait()
    gu = jnp.zeros((256, C), F32)
    for i in range(9):
        for e in range(3):
            gu += lax.dot_general(
                shifted(gyep, i, slice(e * C, e * C + C)), w[i * 1152 + e * C : i * 1152 + e * C + C, :],
                (((1,), (1,)), ((), ())), preferred_element_type=F32)

    rr, gn, sg = act(hf[...])
    gv = gu * sg * (1.0 + gn * (1.0 - sg))
    gh = gyef[:, C : 2 * C] + rr * (gv - gn * jnp.mean(gv * gn, axis=-1, keepdims=True))
    hf[...] = gh
    ghs[...] = jnp.zeros_like(ghs)
    for cc in range(4):
        ghs[0:64, cc * C : cc * C + C] = jnp.concatenate(
            [hf[(fr * 4 + cc) * 8 : (fr * 4 + cc) * 8 + 8, :] for fr in range(8)], axis=0).astype(BF)
    xst = xsf[...].T.astype(BF)
    gif[...] = jnp.zeros_like(gif)
    for a in range(3):
        df[...] = jnp.dot(xst, ghs[(2 - a) * 32 : (2 - a) * 32 + 64, :], preferred_element_type=F32)
        for b in range(3):
            for e in range(3):
                total = jnp.zeros((16, C), F32)
                for cc in range(4):
                    ci = cc + e - 1
                    if 0 <= ci < 4:
                        total += df[(b * 4 + ci) * 16 : (b * 4 + ci) * 16 + 16, cc * C : cc * C + C]
                gif[(a * 9 + b * 3 + e) * 16 : (a * 9 + b * 3 + e) * 16 + 16, :] = total
    for blk in range(8):
        at = 16 * ((27 * blk) // 8)
        gib[blk % 2, blk // 2] = gif[at : at + GROWS, :].astype(BF)

    def icore():
        return pltpu.make_async_remote_copy(
            gib.at[1 - c], rgi, i_send.at[0], i_recv.at[0], device_id=sib, device_id_type=MESH)

    base = load * 54 - 16 * ((27 * load) // 8)

    def xstart(v):
        return al(16 * ((2 * base + 27 * v) // 32), 16)

    def ipeer(axis, d):
        v = lax.rem(pos[axis] + d, 4)
        src, dst, k = {
            "z": (gzb.at[v], rz.at[d - 1], 0),
            "x": (gxb.at[pl.ds(xstart(v), 32)], rx.at[d - 1], 3),
            "y": (gyb, ry.at[d - 1], 6),
        }[axis]
        return pltpu.make_async_remote_copy(
            src, dst, i_send.at[k + d], i_recv.at[k + d], device_id=dev(axis, v), device_id_type=MESH)

    def in_z():
        icore().wait_recv()
        for zz in range(4):
            at = al(16 * ((27 * (zz * 2 + c)) // 8), 16)
            total = gif[pl.ds(at, GROWS), :] + rgi[zz].astype(F32)
            gz[zz] = total
            gzb[zz] = total.astype(BF)
        for d in range(1, 4):
            ipeer("z", d).start()

    def in_x():
        for d in range(1, 4):
            ipeer("z", d).wait_recv()
        total = gz[z] + rz[0].astype(F32) + rz[1].astype(F32) + rz[2].astype(F32)
        gx[...] = total
        gxb[...] = total.astype(BF)
        for d in range(1, 4):
            ipeer("x", d).start()

    def in_y():
        for d in range(1, 4):
            ipeer("x", d).wait_recv()
        total = gx[pl.ds(xstart(x), 32), :] + rx[0].astype(F32) + rx[1].astype(F32) + rx[2].astype(F32)
        gyv[...] = total
        gyb[...] = total.astype(BF)
        for d in range(1, 4):
            ipeer("y", d).start()

    def in_end():
        for d in range(1, 4):
            ipeer("y", d).wait_recv()
        total = gyv[...] + ry[0].astype(F32) + ry[1].astype(F32) + ry[2].astype(F32)
        fg[96:, :] = jnp.zeros((8, 128), F32)
        for j in range(3):
            fg[pl.ds(j, 32, stride=3), :] = total[:, j * 128 : j * 128 + 128]
        first = 384 * (base - 16 * ((2 * base + 27 * x) // 32)) + 1296 * q
        at, lo = first // 128, lax.rem(first, 128)
        shift = lax.rem(128 - lo, 128)
        head = pltpu.roll(fg[pl.ds(at, 16), :], shift, 1)
        tail = pltpu.roll(fg[pl.ds(at + 1, 16), :], shift, 1)
        gin_ref[...] = jnp.where(iota((16, 128), 1) < 128 - lo, head, tail)

    icore().start()
    relay(((1, 0), (2, 0)))

    @pl.loop(1, 16)
    def _(d):
        afrom(d).wait_recv()

    dst, src = iota((256, 256), 0), iota((256, 256), 1)
    order = (dst // 32 == (src // 2) % 8) & ((dst // 2) % 16 == src // 16) & (dst % 2 == src % 2)
    xbf[...] = jnp.dot(jnp.where(order, 1.0, 0.0).astype(BF), rcv[...], preferred_element_type=F32)
    xbp[0:256, :] = jnp.zeros((256, 256), BF)
    xbp[256:512, :] = xbf[...].astype(BF)
    ud[...] = jnp.zeros_like(ud)
    for f in range(2):
        hd = jnp.dot(xbp[f * 128 : f * 128 + 128, :], we[0:256, :], preferred_element_type=F32)
        hd += jnp.dot(xbp[f * 128 + 128 : f * 128 + 256, :], we[256:512, :], preferred_element_type=F32)
        hd += jnp.dot(xbp[f * 128 + 256 : f * 128 + 384, :], we[512:768, :], preferred_element_type=F32)
        for cc in range(4):
            hc = hd[:, cc * C : cc * C + C]
            _, gc, sc = act(hc)
            uc = (gc * sc).astype(BF)
            for r in range(4):
                rows = slice(r * 32, r * 32 + 32)
                acc[((f * 4 + r) * 4 + cc) * 32 : ((f * 4 + r) * 4 + cc) * 32 + 32, :] = hc[rows]
                to = (f + 2) * 512 + r * 128 + cc * 32
                for e in range(3):
                    if 0 <= cc - e + 1 < 4:
                        ud[to + (1 - e) * 32 : to + (1 - e) * 32 + 32, e * C : e * C + C] = uc[rows]

    relay(((0, 0), (1, 1), (2, 1)))
    in_z()

    def decode(a, f):
        taps = jnp.concatenate([w[(a * 3 + b) * 1152 : (a * 3 + b) * 1152 + 1152, :] for b in range(3)], axis=1)
        out = jnp.dot(ud[(f + a) * 512 : (f + a) * 512 + 512, :], taps, preferred_element_type=F32)
        top = f * 512
        acc[top + 128 : top + 512, :] += out[0:384, 0:C]
        acc[top : top + 512, :] += out[:, C : 2 * C]
        acc[top : top + 384, :] += out[128:512, 2 * C :]

    def emit(f):
        for p in range(16 * f, 16 * f + 16):
            m = xbf[p // 4 * 32 : p // 4 * 32 + 32, 192 + p % 4 : 193 + p % 4]
            dec_ref[:, p * C : p * C + C] = (acc[p * 32 : p * 32 + 32, :] * m).astype(BF)
        store(f).start()

    decode(0, 0)
    decode(0, 1)
    second()
    in_x()
    decode(1, 0)
    decode(1, 1)
    third()
    in_y()
    decode(2, 0)
    emit(0)
    decode(2, 1)
    emit(1)
    finish()
    in_end()

    @pl.loop(1, 16)
    def _(d):
        acopy(d).wait_send()

    store(0).wait()
    store(1).wait()
    swap(0).wait_send()
    swap(1).wait_send()
    for j in range(3):
        for n in range(6):
            for r in range(PIECES[j]):
                ring(j, n, r).wait_send()
        for d in range(1, 4):
            direct(j, 1, d).wait_send()
            direct(j, 2, d).wait_send()
    icore().wait_send()
    for axis in ("z", "x", "y"):
        for d in range(1, 4):
            ipeer(axis, d).wait_send()


def deliver(d_ref, i_ref, m_ref, dec_ref, gin_ref, gmid_ref, d_buf, i_buf, m_buf, sem):
    ins = [pltpu.make_async_copy(a, b, sem.at[n]) for n, (a, b) in enumerate(
        ((i_ref, i_buf), (m_ref, m_buf), (d_ref.at[:, 0:6144], d_buf.at[:, 0:6144]),
         (d_ref.at[:, 6144:], d_buf.at[:, 6144:])))]
    for copy in ins:
        copy.start()
    ins[0].wait()
    for n in range(10):
        gin_ref[pl.ds(n * 128, 128)] = i_buf[n, :] * FACTOR
    gin_ref[pl.ds(1280, 16)] = i_buf[10, 0:16] * FACTOR
    ins[1].wait()
    m_buf[...] = m_buf[...] * FACTOR
    outs = [pltpu.make_async_copy(a, b, sem.at[4 + n]) for n, (a, b) in enumerate(
        ((m_buf, gmid_ref), (d_buf.at[:, 0:6144], dec_ref.at[:, 0:6144]), (d_buf.at[:, 6144:], dec_ref.at[:, 6144:])))]
    outs[0].start()
    for n in (1, 2):
        ins[n + 1].wait()
        outs[n].start()
    for copy in outs:
        copy.wait()


def shards(latents, cotangent, frames, heights, widths, bucket_ids, w_in, w_mid):
    v = pltpu.VMEM
    dma = pltpu.SemaphoreType.DMA
    vm = pl.BlockSpec(memory_space=pltpu.VMEM)
    sm = pl.BlockSpec(memory_space=pltpu.SMEM)
    hbm = pl.BlockSpec(memory_space=pl.ANY)
    dec, gin, gmid = pl.pallas_call(
        kernel,
        out_shape=(
            jax.ShapeDtypeStruct((32, 12288), BF),
            jax.ShapeDtypeStruct((16, 128), F32),
            jax.ShapeDtypeStruct((243, 128), F32),
        ),
        in_specs=[sm, sm, sm, sm, hbm, hbm, hbm, hbm],
        out_specs=(hbm, vm, vm),
        scratch_shapes=[
            v((10368, C), BF), v((768, 1536), BF), v((256, 256), BF), v((256, 256), BF), v((64, 256), F32),
            v((128, 256), BF), v((256, 256), F32), v((512, 256), BF), v((256, C), F32),
            v((256, C), BF), v((256, C), BF), v((256, C), BF), v((256, C), BF), v((256, 1152), F32),
            v((1152, 512), BF), v((256, 1152), F32), v((768, 1152), BF), v((768, C), BF), v((128, 1536), BF),
            v((256, 1536), F32), v((448, C), F32), v((2, 4, GROWS, C), BF), v((4, GROWS, C), BF),
            v((4, GROWS, C), F32), v((4, GROWS, C), BF), v((3, GROWS, C), BF), v((GROWS, C), F32), v((GROWS, C), BF),
            v((3, 32, C), BF), v((32, C), F32), v((32, C), BF), v((3, 32, C), BF), v((3, 4, ROWS, 128), BF),
            v((64, PIECE, 128), BF),
            v((656, 128), BF), v((640, 128), BF), v((ROWS, 128), BF), v((ROWS, 128), BF),
            v((2, 336, 128), BF), v((2, 336, 128), BF), v((4, 336, 128), BF), v((4, 336, 128), BF),
            v((8, PIECE, 128), BF), v((8, PIECE, 128), BF), v((16, PIECE, 128), BF), v((16, PIECE, 128), BF),
            v((48, PIECE, 128), F32), v((48, PIECE, 128), BF), v((9, 4, PIECE, 128), BF), v((12, PIECE, 128), F32),
            v((9, PIECE, 128), F32), v((3, PIECE + 8, 128), F32), v((264, 128), F32), v((104, 128), F32),
            v((2048, 1152), BF), v((1024, C), F32), v((8, 512), BF), v((8, 12288), BF), v((432, C), BF), v((32, 12288), BF),
            dma((5,)), dma((9,)), dma((16,)), dma((16,)), dma((2,)), dma((2,)), dma((36,)), dma((36,)), dma((18,)), dma((18,)),
            dma((10,)), dma((10,)),
        ],
        compiler_params=pltpu.CompilerParams(
            collective_id=0, has_side_effects=True, vmem_limit_bytes=62 * 1024 * 1024),
    )(bucket_ids, frames, heights, widths, latents, cotangent, w_in, w_mid)
    dec, gin, gmid = pl.pallas_call(
        deliver,
        out_shape=(
            jax.ShapeDtypeStruct((32, 12288), BF),
            jax.ShapeDtypeStruct((1296,), F32),
            jax.ShapeDtypeStruct((243, 128), F32),
        ),
        in_specs=[hbm, hbm, hbm],
        out_specs=(hbm, vm, hbm),
        scratch_shapes=[v((32, 12288), BF), v((16, 128), F32), v((243, 128), F32), dma((7,))],
    )(dec, gin, gmid)
    return (dec, gin, gmid.reshape(-1))


def solution(mesh):
    return jax.shard_map(
        shards,
        mesh=mesh,
        in_specs=(
            P(("loader", "bucket"), None),
            P(("loader", "bucket"), None),
            P(("loader", "bucket")),
            P(("loader", "bucket")),
            P(("loader", "bucket")),
            P(("loader", "bucket")),
            P(),
            P(),
        ),
        out_specs=(P(("loader", "bucket"), None), P(("loader", "bucket")), P(("loader", "bucket"))),
        check_vma=False,
    )
```
